128 devices in a mesh: ctx: 16 (over y, x), tp: 8 (over z, core).
Axes of the slice: x: 4, y: 4, z: 4, core: 2. Of those that a mesh axis runs over, the one named last changes fastest.
Arguments:
- tokens_in: bfloat16 [4096, 8192], P('ctx', 'tp'), may hold values from -6 to 6
- base_queries: bfloat16 [4096, 8192], P('ctx', 'tp'), may hold values from -6 to 6
- fresh_keys: bfloat16 [4096, 1024], P('ctx', 'tp'), may hold values from -6 to 6
- fresh_values: bfloat16 [4096, 1024], P('ctx', 'tp'), may hold values from -6 to 6
- cached_key_rows: bfloat16 [16384, 1024], P('ctx', 'tp'), may hold values from -6 to 6
- cached_value_rows: bfloat16 [16384, 1024], P('ctx', 'tp'), may hold values from -6 to 6
- adapter_store: bfloat16 [64, 2, 64, 8192], P('ctx', None, None, 'tp'), may hold values from -0.125 to 0.125
- adapter_slot: int32 [64], replicated, may hold values from 0 to 63, each once
- segment_adapter: int32 [17], replicated, may hold values from 0 to 63
- token_request: int32 [4096], P('ctx'), may hold values from 0 to 16, as said below
- cache_doc: int32 [128], P('ctx'), may hold values from 0 to 16
Outputs:
- attended: bfloat16 [4096, 8192], P('ctx', 'tp')
The draws below stay inside these ranges and needn't reach their ends.
Inputs may be any that keep to these rules, and one draw needn't show every extreme that they name: `token_request`: segment ids never fall; each aligned block of 256 tokens begins inside the segment that began in the block before (the first block with segment 0) and starts exactly one new segment, at a position of 1 to 254 of the block.
All inputs are finite; a program needn't handle non-finite values.
Results may differ from the reference program's by a relative error of at most 0.024.
Values may be sent and summed in bfloat16 or wider, within the bound.
No kernel may reach another device: no remote copies, remote signals or barrier semaphores. Data moves between devices by JAX's collectives and lax.ppermute only.
A program may use at most 128 MiB of HBM per device.

```python
import math
import jax
import jax.numpy as jnp
import numpy as np
from jax import lax

MODEL_WIDTH = 8192
QUERY_HEADS = 64
KEY_VALUE_HEADS = 8
HEAD_SIZE = 128
R = 64
ADAPTERS = 64
PAGE = 128
TOKENS_PER_SHARD = 256
SPAN_TOKENS = 4096
CACHED_TOTAL = 16384
CACHE_PAGES = 128
SEGS = 17


def draw_base_queries(key, part):
    key = jax.random.fold_in(key, 5)
    output_values = jnp.clip(jax.random.normal(key, (SPAN_TOKENS, QUERY_HEADS * HEAD_SIZE), jnp.float32), -6.0, 6.0)
    return output_values.astype(jnp.bfloat16)


def draw_fresh_keys(key, part):
    key = jax.random.fold_in(key, 7)
    output_values = jnp.clip(jax.random.normal(key, (SPAN_TOKENS, KEY_VALUE_HEADS * HEAD_SIZE), jnp.float32), -6.0, 6.0)
    return output_values.astype(jnp.bfloat16)


def draw_token_request(key, part):
    key = jax.random.fold_in(key, 9)
    blocks = SPAN_TOKENS // TOKENS_PER_SHARD
    starts = jax.random.randint(key, (blocks,), 1, TOKENS_PER_SHARD - 1)
    position = jnp.arange(SPAN_TOKENS)
    block_index = position // TOKENS_PER_SHARD
    inside = position % TOKENS_PER_SHARD
    return (block_index + (inside >= starts[block_index]).astype(jnp.int32)).astype(jnp.int32)


def draw_cache_doc(key, part):
    key = jax.random.fold_in(key, 11)
    key_pair, key_order, key_side, key_rest = jax.random.split(key, 4)
    heavy_first = jax.random.randint(key_pair, (), 0, SEGS - 1)
    page_order = jax.random.permutation(key_order, CACHE_PAGES)
    heavy_count = 3 * CACHE_PAGES // 4
    side_pick = jax.random.randint(key_side, (CACHE_PAGES,), 0, 2)
    spread_owner = jax.random.randint(key_rest, (CACHE_PAGES,), 0, SEGS)
    return jnp.where(page_order < heavy_count, heavy_first + side_pick, spread_owner).astype(jnp.int32)


def with_ends(drawn, own_key, low, top_value):
    longest = drawn.shape.index(max(drawn.shape))
    spots = []
    for shift in (0, 1):
        where = [jax.random.randint(jax.random.fold_in(own_key, axis), (), 0, length) for axis, length in enumerate(drawn.shape)]
        where[longest] = (where[longest] + shift) % drawn.shape[longest]
        spots.append(tuple(where))
    return drawn.at[spots[0]].set(low).at[spots[1]].set(top_value)


def level_of(rng, extent, shards, smallest, high):
    loudness, own = 1.0, jax.random.fold_in(rng, 6)
    for dim, blocks in shards:
        steps = jnp.exp(jax.random.uniform(jax.random.fold_in(own, dim), (blocks,), jnp.float32, smallest / len(shards), high / len(shards)))
        loudness = loudness * jnp.repeat(steps, extent[dim] // blocks).reshape([-1 if axis == dim else 1 for axis in range(len(extent))])
    return loudness


def rank_bounds(amount, lean):
    loads = [(1 << 20) // math.isqrt(grade ** lean) + 1 for grade in range(1, amount + 1)]
    scale = 1 + sum(loads) // (1 << 30)
    return np.cumsum(np.array([max(1, weight // scale) for weight in loads]))


def skewed_ids(key, shape, count, lean):
    table = rank_bounds(count, lean)
    lot = jax.random.randint(jax.random.fold_in(key, 1), shape, 0, int(table[count - 1]))
    standing = jnp.searchsorted(jnp.asarray(table, jnp.int32), lot, side="right")
    return jax.random.permutation(jax.random.fold_in(key, 2), count)[standing].astype(jnp.int32)


def normal_values(rng, extent, deviation, most, cuts=(), kind=jnp.bfloat16):
    level = level_of(rng, extent, cuts, -0.22, 0.18) if cuts else 1.0
    array = jax.random.normal(rng, extent, jnp.float32) * deviation * level
    return jnp.minimum(jnp.maximum(array, -most), most).astype(kind)


def setup_inputs(seed: int = 0) -> dict:
    key_list = jax.random.split(jax.random.key(seed), 12)
    return {
        "tokens_in": normal_values(key_list[0], (SPAN_TOKENS, MODEL_WIDTH), 1.0, 6.0, ((0, 16), (1, 8))),
        "base_queries": draw_base_queries(jax.random.fold_in(key_list[11], 71), 0),
        "fresh_keys": draw_fresh_keys(jax.random.fold_in(key_list[11], 71), 0),
        "fresh_values": normal_values(key_list[3], (SPAN_TOKENS, KEY_VALUE_HEADS * HEAD_SIZE), 1.0, 6.0, ((0, 16), (1, 8))),
        "cached_key_rows": normal_values(key_list[4], (CACHED_TOTAL, KEY_VALUE_HEADS * HEAD_SIZE), 1.0, 6.0, ((0, 16), (1, 8))),
        "cached_value_rows": normal_values(key_list[5], (CACHED_TOTAL, KEY_VALUE_HEADS * HEAD_SIZE), 1.0, 6.0, ((0, 16), (1, 8))),
        "adapter_store": normal_values(key_list[6], (ADAPTERS, 2, R, MODEL_WIDTH), (R * 32) ** -0.5, 0.125, ((0, 16), (3, 8))),
        "adapter_slot": jax.random.permutation(key_list[7], ADAPTERS).astype(jnp.int32),
        "segment_adapter": with_ends(skewed_ids(key_list[8], (SEGS,), ADAPTERS, 2), jax.random.fold_in(key_list[8], 3), 0, ADAPTERS - 1).astype(jnp.int32),
        "token_request": draw_token_request(jax.random.fold_in(key_list[11], 71), 0),
        "cache_doc": draw_cache_doc(jax.random.fold_in(key_list[11], 71), 0),
    }


adapter_scale = 2.0


def reference(tokens_in, base_queries, fresh_keys, fresh_values, cached_key_rows, cached_value_rows, adapter_store, adapter_slot, segment_adapter, token_request, cache_doc):
    adapter_term = jnp.zeros((SPAN_TOKENS, MODEL_WIDTH), jnp.float32)
    for request_segment in range(SEGS):
        store_row = adapter_slot[segment_adapter[request_segment]]
        block = adapter_store[store_row]
        rank_acts = jnp.dot(tokens_in, block[0].T, preferred_element_type=jnp.float32)
        rank_round = rank_acts.astype(jnp.bfloat16)
        matrix_product = jnp.dot(rank_round, block[1], preferred_element_type=jnp.float32)
        adapter_term = adapter_term + jnp.where((token_request == request_segment)[:, None], matrix_product, 0.0)
    query_rows = (base_queries.astype(jnp.float32) + adapter_scale * adapter_term).astype(jnp.bfloat16)
    group_width = QUERY_HEADS // KEY_VALUE_HEADS
    score_scale = 1.0 / (HEAD_SIZE ** 0.5)
    doc_rows = jnp.repeat(cache_doc, PAGE)
    key_matrix = jnp.concatenate([cached_key_rows, fresh_keys], axis=0).reshape(CACHED_TOTAL + SPAN_TOKENS, KEY_VALUE_HEADS, HEAD_SIZE)
    value_matrix = jnp.concatenate([cached_value_rows, fresh_values], axis=0).reshape(CACHED_TOTAL + SPAN_TOKENS, KEY_VALUE_HEADS, HEAD_SIZE)
    key_segment = jnp.concatenate([doc_rows, token_request]).astype(jnp.int32)
    key_place = jnp.concatenate([jnp.full((CACHED_TOTAL,), -1, jnp.int32), jnp.arange(SPAN_TOKENS, dtype=jnp.int32)])
    query_tiles = query_rows.reshape(SPAN_TOKENS // TOKENS_PER_SHARD, TOKENS_PER_SHARD, KEY_VALUE_HEADS, group_width, HEAD_SIZE)
    segment_blocks = token_request.reshape(SPAN_TOKENS // TOKENS_PER_SHARD, TOKENS_PER_SHARD)
    place_blocks = jnp.arange(SPAN_TOKENS, dtype=jnp.int32).reshape(SPAN_TOKENS // TOKENS_PER_SHARD, TOKENS_PER_SHARD)

    def attend_block(block_args):
        query_part, segment_part, place_part = block_args
        visible = (key_segment[None, :] == segment_part[:, None]) & (key_place[None, :] <= place_part[:, None])
        head_outs = []
        for group_offset in range(KEY_VALUE_HEADS):
            scores = jnp.einsum('tcd,nd->tcn', query_part[:, group_offset].astype(jnp.float32), key_matrix[:, group_offset].astype(jnp.float32)) * score_scale
            masked = jnp.where(visible[:, None, :], scores, -jnp.inf)
            row_max = jnp.max(masked, axis=-1, keepdims=True)
            weights = jnp.where(visible[:, None, :], jnp.exp(scores - row_max), 0.0)
            row_sum = jnp.sum(weights, axis=-1)
            weight_round = lax.optimization_barrier(weights.astype(jnp.bfloat16))
            summed = jnp.einsum('tcn,nd->tcd', weight_round.astype(jnp.float32), value_matrix[:, group_offset].astype(jnp.float32))
            head_outs.append(summed / row_sum[..., None])
        return jnp.stack(head_outs, axis=1).reshape(TOKENS_PER_SHARD, QUERY_HEADS * HEAD_SIZE).astype(jnp.bfloat16)

    attended = lax.map(attend_block, (query_tiles, segment_blocks, place_blocks))
    return attended.reshape(SPAN_TOKENS, QUERY_HEADS * HEAD_SIZE)
```

```python
import functools
import math

import jax
import jax.numpy as jnp
from jax import lax
from jax.experimental import pallas as pl
from jax.experimental.pallas import tpu as pltpu
from jax.sharding import PartitionSpec as P

HEAD_SIZE = 128
PAGE = 128
SIDE = 4
HALF_ROWS = 1040
TILE = 32
GROUP = 4
VMEM_LIMIT = 56 * 1024 * 1024

adapter_scale = 2.0


def pull(block, dx, dy):
    route = []
    for i in range(SIDE * SIDE):
        y, x = divmod(i, SIDE)
        route.append((((y + dy) % SIDE) * SIDE + (x + dx) % SIDE, i))
    return lax.ppermute(block, "ctx", route)


def pull_tp(block, dz, dc):
    route = []
    for i in range(2 * SIDE):
        z, c = divmod(i, 2)
        route.append((((z + dz) % SIDE) * 2 + (c ^ dc), i))
    return lax.ppermute(block, "tp", route)


def pick_kernel(index_ref, b0, b1, b2, b3, o0, o1, o2, o3, sems):
    bufs, outs = (b0, b1, b2, b3), (o0, o1, o2, o3)
    for k in range(8):
        index = index_ref[k]
        row = lax.rem(index, 4)
        for b in range(4):
            @pl.when(index // 4 == b)
            def _():
                pltpu.make_async_copy(bufs[b].at[row], outs[k // 2].at[k % 2], sems.at[k]).start()
    for k in range(8):
        pltpu.make_async_copy(bufs[0].at[0], outs[k // 2].at[k % 2], sems.at[k]).wait()


def pick(index, bufs):
    rank, width = bufs[0].shape[1:]
    out = jax.ShapeDtypeStruct((2, rank, width), jnp.bfloat16)
    return pl.pallas_call(
        pick_kernel,
        out_shape=[out] * 4,
        in_specs=[pl.BlockSpec(memory_space=pltpu.SMEM)] + [pl.BlockSpec(memory_space=pl.ANY)] * 4,
        out_specs=[pl.BlockSpec(memory_space=pl.ANY)] * 4,
        scratch_shapes=[pltpu.SemaphoreType.DMA((8,))],
        name="pick_items",
    )(index, *bufs)


def route_adapter(raw, rows_of, me_along, me_across, along_x):
    def first(v, d):
        return pull(v, d, 0) if along_x else pull(v, 0, d)

    def second(v, d):
        return pull(v, 0, d) if along_x else pull(v, d, 0)

    ring = [raw, first(raw, 1), first(raw, 2), first(raw, -1)]
    index = []
    for d in range(4):
        there = (me_across + d) % SIDE
        dest = there * SIDE + me_along if along_x else me_along * SIDE + there
        for k in range(2):
            row = rows_of[dest + k]
            owner = row // 4
            owner_along = owner % SIDE if along_x else owner // SIDE
            index.append(((owner_along - me_along + SIDE) % SIDE) * 4 + row % 4)
    items = pick(jnp.stack(index).astype(jnp.int32), ring)
    got = [items[0], second(items[3], 1), second(items[2], 2), second(items[1], -1)]
    me = me_across * SIDE + me_along if along_x else me_along * SIDE + me_across
    blocks = []
    for k in range(2):
        owner = rows_of[me + k] // 4
        owner_across = owner // SIDE if along_x else owner % SIDE
        source = (owner_across - me_across + SIDE) % SIDE
        block = got[0][k]
        for d in range(1, 4):
            block = jnp.where(source == d, got[d][k], block)
        blocks.append(block)
    return jnp.concatenate(blocks, axis=0)


def spread(own):
    east, west = pull(own, 1, 0), pull(own, -1, 0)
    south, north = pull(own, 0, 1), pull(own, 0, -1)
    lo = lambda v: v[0:1]
    hi = lambda v: v[1:2]
    join = lambda *v: jnp.concatenate(v, axis=0)
    e2 = pull(join(lo(east), lo(south), hi(north)), 1, 0)
    w2 = pull(join(hi(west), hi(south), lo(north)), -1, 0)
    s2 = pull(join(lo(south), hi(east), lo(west)), 0, 1)
    n2 = pull(join(hi(north), lo(east), hi(west)), 0, -1)
    e3, w3 = pull(e2[1:], 1, 0), pull(w2[1:], -1, 0)
    s3, n3 = pull(s2[1:], 0, 1), pull(n2[1:], 0, -1)
    e4 = pull(n3[0:1], 1, 0)
    s4 = pull(w3[0:1], 0, 1)
    return (own, east, west, south, north), (e2, w2, s2, n2), (e3, w3, s3, n3), (e4, s4)


def owners(bufs):
    return jnp.concatenate([b[:, 1024, :4].reshape(-1) for b in bufs]).astype(jnp.int32)


LOG_SCALE = math.log2(math.e) / math.sqrt(HEAD_SIZE)


def soft_step(q, keys, values, m_ref, al_ref, rows, mask=None):
    scores = lax.dot_general(q, keys, (((1,), (1,)), ((), ())), preferred_element_type=jnp.float32)
    scores = scores * LOG_SCALE
    if mask is not None:
        scores = jnp.where(mask, scores, -1e30)
    count = scores.shape[1] // 128
    parts = [scores[:, i * 128:(i + 1) * 128] for i in range(count)]
    peak = functools.reduce(jnp.maximum, parts)
    peak = jnp.max(peak, axis=1, keepdims=True)
    old = m_ref[rows, :]
    new = jnp.maximum(old, peak)
    fade = jnp.exp2(old - new)
    weights = jnp.concatenate([jnp.exp2(s - new).astype(jnp.bfloat16) for s in parts], axis=1)
    added = jnp.dot(weights, values, preferred_element_type=jnp.float32)
    m_ref[rows, :] = new
    al_ref[rows, 0:128] = al_ref[rows, 0:128] * fade + added[:, 0:128]
    al_ref[rows, 128:256] = al_ref[rows, 128:256] * fade + added[:, 128:256]


def attend_kernel(first, last, sizes, *refs):
    info_ref, q_ref = refs[0], refs[1]
    pos = 2
    if first:
        span_ref, prev_ref = refs[pos:pos + 2]
        pos += 2
    else:
        m_in, al_in = refs[pos:pos + 2]
        pos += 2
    bufs = refs[pos:pos + len(sizes)]
    pos += len(sizes)
    if last:
        out_ref = refs[pos]
        pos += 1
    else:
        m_out, al_out = refs[pos:pos + 2]
        pos += 2
    k_sc, v_sc, count_sc, m_sc, al_sc, m_keep, al_keep = refs[pos:]
    rows_tile = TILE * 8
    tiles = q_ref.shape[0] // rows_tile
    seg_a, cut, prev_cut = info_ref[0], info_ref[1], info_ref[2]

    if first:
        m_sc[...] = jnp.full(m_sc.shape, -1e30, jnp.float32)
        al_sc[...] = jnp.zeros(al_sc.shape, jnp.float32)
        v_sc[0, :, 128:256] = jnp.ones((v_sc.shape[1], 128), jnp.bfloat16)
        v_sc[0, 0:256, 0:128] = prev_ref[256:512, :]
        v_sc[0, 256:512, 0:128] = span_ref[256:512, :]
        k_sc[0, 0:256, :] = prev_ref[0:256, :]
        k_sc[0, 256:512, :] = span_ref[0:256, :]

        @pl.loop(0, tiles)
        def _(t):
            rows = pl.ds(pl.multiple_of(t * rows_tile, rows_tile), rows_tile)
            token = t * TILE + lax.broadcasted_iota(jnp.int32, (rows_tile, 512), 0) % TILE
            key = lax.broadcasted_iota(jnp.int32, (rows_tile, 512), 1) - 256
            in_a = token < cut
            mask = ((key < 0) & in_a & (key + 256 >= prev_cut)) | (
                (key >= 0) & (key <= token) & ((key < cut) == in_a)
            )
            soft_step(q_ref[rows, :], k_sc[0, 0:512, :], v_sc[0, 0:512, :], m_sc, al_sc, rows, mask)
    else:
        m_sc[...] = m_in[...]
        al_sc[...] = al_in[...]

    v_sc[0, :, 128:256] = jnp.ones((v_sc.shape[1], 128), jnp.bfloat16)
    v_sc[1, :, 128:256] = jnp.ones((v_sc.shape[1], 128), jnp.bfloat16)
    count_sc[0] = 0
    count_sc[1] = 0
    base = 3
    for buf, halves in zip(bufs, sizes):
        @pl.loop(0, halves * 4)
        def _(i, buf=buf, base=base):
            which = info_ref[base + i] - seg_a

            @pl.when((which == 0) | (which == 1))
            def _():
                n = count_sc[which]
                there = pl.ds(pl.multiple_of(n * PAGE, PAGE), PAGE)
                h, page = i // 4, i % 4
                k_sc[which, there, :] = buf[h, pl.ds(pl.multiple_of(page * PAGE, PAGE), PAGE), :]
                v_sc[which, there, 0:128] = buf[
                    h, pl.ds(pl.multiple_of(512 + page * PAGE, PAGE), PAGE), :
                ]
                count_sc[which] = n + 1
        base += halves * 4

    for side in range(2):
        n = count_sc[side]
        full = ((n + GROUP - 1) // GROUP) * GROUP

        @pl.loop(n, full)
        def _(i, side=side):
            there = pl.ds(pl.multiple_of(i * PAGE, PAGE), PAGE)
            k_sc[side, there, :] = k_sc[side, 0:PAGE, :]
            v_sc[side, there, :] = jnp.zeros((PAGE, 256), jnp.bfloat16)

        low = 0 if side == 0 else cut // TILE
        high = (cut + TILE - 1) // TILE if side == 0 else tiles
        high = jnp.where(n > 0, high, low)

        @pl.loop(low, high)
        def _(t, side=side, full=full):
            rows = pl.ds(pl.multiple_of(t * rows_tile, rows_tile), rows_tile)
            mixed = (t * TILE < cut) & ((t + 1) * TILE > cut)

            @pl.when(mixed)
            def _():
                m_keep[...] = m_sc[rows, :]
                al_keep[...] = al_sc[rows, :]

            @pl.loop(0, full // GROUP)
            def _(g):
                there = pl.ds(pl.multiple_of(g * (GROUP * PAGE), GROUP * PAGE), GROUP * PAGE)
                soft_step(q_ref[rows, :], k_sc[side, there, :], v_sc[side, there, :], m_sc, al_sc, rows)

            @pl.when(mixed)
            def _():
                token = t * TILE + lax.broadcasted_iota(jnp.int32, (rows_tile, 128), 0) % TILE
                mine = (token < cut) if side == 0 else (token >= cut)
                m_sc[rows, :] = jnp.where(mine, m_sc[rows, :], m_keep[...])
                for c in range(2):
                    cols = slice(c * 128, (c + 1) * 128)
                    al_sc[rows, cols] = jnp.where(mine, al_sc[rows, cols], al_keep[:, cols])

    if last:
        for t in range(tiles):
            for h in range(8):
                rows = slice((t * 8 + h) * TILE, (t * 8 + h + 1) * TILE)
                out = al_sc[rows, 0:128] / al_sc[rows, 128:256]
                out_ref[t * TILE:(t + 1) * TILE, h * 128:(h + 1) * 128] = out.astype(jnp.bfloat16)
    else:
        m_out[...] = m_sc[...]
        al_out[...] = al_sc[...]


def attend(info, q, span, state, bufs, last):
    first = state is None
    sizes = tuple(b.shape[0] for b in bufs)
    pages = 4 * sum(sizes)
    pages = max(((pages + GROUP - 1) // GROUP) * GROUP, 4)
    rows = q.shape[0]
    state_shape = [
        jax.ShapeDtypeStruct((rows, 128), jnp.float32),
        jax.ShapeDtypeStruct((rows, 256), jnp.float32),
    ]
    vmem = pl.BlockSpec(memory_space=pltpu.VMEM)
    args = [info, q] + (list(span) if first else list(state)) + list(bufs)
    out_shape = jax.ShapeDtypeStruct((rows // 8, 1024), jnp.bfloat16) if last else state_shape
    return pl.pallas_call(
        functools.partial(attend_kernel, first, last, sizes),
        out_shape=out_shape,
        in_specs=[pl.BlockSpec(memory_space=pltpu.SMEM)] + [vmem] * (len(args) - 1),
        out_specs=vmem if last else [vmem, vmem],
        scratch_shapes=[
            pltpu.VMEM((2, pages * PAGE, 128), jnp.bfloat16),
            pltpu.VMEM((2, pages * PAGE, 256), jnp.bfloat16),
            pltpu.SMEM((2,), jnp.int32),
            pltpu.VMEM((rows, 128), jnp.float32),
            pltpu.VMEM((rows, 256), jnp.float32),
            pltpu.VMEM((TILE * 8, 128), jnp.float32),
            pltpu.VMEM((TILE * 8, 256), jnp.float32),
        ],
        compiler_params=pltpu.CompilerParams(vmem_limit_bytes=VMEM_LIMIT),
        name="attend_last" if last else ("attend_first" if first else "attend_mid"),
    )(*args)


def per_device(
    tokens_in,
    base_queries,
    fresh_keys,
    fresh_values,
    cached_key_rows,
    cached_value_rows,
    adapter_store,
    adapter_slot,
    segment_adapter,
    token_request,
    cache_doc,
):
    tok_rows = tokens_in.shape[0]
    me = lax.axis_index("ctx")
    me_y, me_x = me // SIDE, me % SIDE
    rows_of = adapter_slot[segment_adapter]
    seg_a = token_request[0]
    cut = jnp.sum((token_request == seg_a).astype(jnp.int32))

    down = route_adapter(adapter_store[:, 0], rows_of, me_x, me_y, True)
    up = route_adapter(adapter_store[:, 1], rows_of, me_y, me_x, False)

    def half(k):
        ids = jnp.pad(cache_doc[k * 4:k * 4 + 4], (0, 124)).astype(jnp.bfloat16)
        return jnp.concatenate(
            [
                cached_key_rows[k * 512:(k + 1) * 512],
                cached_value_rows[k * 512:(k + 1) * 512],
                jnp.broadcast_to(ids[None], (16, 128)),
            ],
            axis=0,
        )

    own = jnp.stack([half(0), half(1)])
    stages = spread(own)
    span = jnp.concatenate(
        [fresh_keys, fresh_values, jnp.broadcast_to(cut.astype(jnp.bfloat16), (16, 128))], axis=0
    )
    prev = lax.ppermute(span, "ctx", [(i - 1, i) for i in range(1, SIDE * SIDE)])
    prev_cut = jnp.where(me == 0, tok_rows, prev[512, 0].astype(jnp.int32))

    in_a = (jnp.arange(tok_rows) < cut)[:, None]
    acts = jnp.dot(tokens_in, down.T, preferred_element_type=jnp.float32)
    acts = jnp.where(in_a, acts[:, :64], acts[:, 64:]).astype(jnp.bfloat16)
    acts = jnp.concatenate([acts[:tok_rows // 2], acts[tok_rows // 2:]], axis=1)
    acts = (acts.astype(jnp.float32) + pull_tp(acts, 0, 1).astype(jnp.float32)).astype(jnp.bfloat16)
    total = acts.astype(jnp.float32)
    for dz in (1, 2, 3):
        total = total + pull_tp(acts, dz, 0).astype(jnp.float32)
    total = jnp.concatenate([total[:, :64], total[:, 64:]], axis=0).astype(jnp.bfloat16)
    zero = jnp.zeros_like(total)
    total = jnp.concatenate([jnp.where(in_a, total, zero), jnp.where(in_a, zero, total)], axis=1)
    lora = jnp.dot(total, up, preferred_element_type=jnp.float32)
    query = (base_queries.astype(jnp.float32) + adapter_scale * lora).astype(jnp.bfloat16)
    query = query.reshape(tok_rows // TILE, TILE, 8, HEAD_SIZE).transpose(0, 2, 1, 3)
    query = query.reshape(tok_rows * 8, HEAD_SIZE)

    def info(bufs):
        return jnp.concatenate([jnp.stack([seg_a, cut, prev_cut]), owners(bufs)])

    state = attend(info(stages[0]), query, (span, prev), None, stages[0], False)
    state = attend(info(stages[1]), query, None, state, stages[1], False)
    late = stages[2] + stages[3]
    return attend(info(late), query, None, state, late, True)


def solution(mesh):
    in_specs = (
        P("ctx", "tp"),
        P("ctx", "tp"),
        P("ctx", "tp"),
        P("ctx", "tp"),
        P("ctx", "tp"),
        P("ctx", "tp"),
        P("ctx", None, None, "tp"),
        P(),
        P(),
        P("ctx"),
        P("ctx"),
    )
    out_specs = P("ctx", "tp")
    return jax.shard_map(
        per_device, mesh=mesh, in_specs=in_specs, out_specs=out_specs, check_vma=False
    )
```

```python
import functools
import math

import jax
import jax.numpy as jnp
from jax import lax
from jax.experimental import pallas as pl
from jax.experimental.pallas import tpu as pltpu
from jax.sharding import PartitionSpec as P

HEAD_SIZE = 128
PAGE = 128
SIDE = 4
RANK = 64
HEADS = 8
TILE = 64
GROUP = 8
STEP_ROWS = TILE * HEADS
NEG = -1e30
VMEM_LIMIT = 56 * 1024 * 1024
LOG_SCALE = math.log2(math.e) / math.sqrt(HEAD_SIZE)

adapter_scale = 2.0


def pull(block, dx, dy):
    route = []
    for i in range(SIDE * SIDE):
        y, x = divmod(i, SIDE)
        route.append((((y + dy) % SIDE) * SIDE + (x + dx) % SIDE, i))
    return lax.ppermute(block, "ctx", route)


def pull_tp(block, dz, dc):
    route = []
    for i in range(2 * SIDE):
        z, c = divmod(i, 2)
        route.append((((z + dz) % SIDE) * 2 + (c ^ dc), i))
    return lax.ppermute(block, "tp", route)


def stored_row(slot_ref, segment_ref, segment):
    return slot_ref[segment_ref[segment]]


def place(index, along_x):
    y, x = index // SIDE, lax.rem(index, SIDE)
    return (x, y) if along_x else (y, x)


def pick_kernel(meta_ref, slot_ref, segment_ref, *refs):
    bufs, outs, sems = refs[0:8], refs[8:16], refs[16]
    me = meta_ref[0]
    for f, along_x in enumerate((True, False)):
        along, across = place(me, along_x)
        for d in range(SIDE):
            there = lax.rem(across + d, SIDE)
            dest = there * SIDE + along if along_x else along * SIDE + there
            for k in range(2):
                row = stored_row(slot_ref, segment_ref, dest + k)
                owner_along, _ = place(row // 4, along_x)
                ring = lax.rem(owner_along - along + SIDE, SIDE)
                for b in range(SIDE):
                    @pl.when(ring == b)
                    def _():
                        pltpu.make_async_copy(
                            bufs[f * 4 + b].at[lax.rem(row, 4)],
                            outs[f * 4 + d].at[k],
                            sems.at[f * 8 + d * 2 + k],
                        ).start()
    for f in range(2):
        for d in range(SIDE):
            for k in range(2):
                pltpu.make_async_copy(
                    bufs[f * 4].at[0], outs[f * 4 + d].at[k], sems.at[f * 8 + d * 2 + k]
                ).wait()


def pick(meta, slot, segment, bufs):
    out = jax.ShapeDtypeStruct((2,) + bufs[0].shape[1:], jnp.bfloat16)
    smem = pl.BlockSpec(memory_space=pltpu.SMEM)
    return pl.pallas_call(
        pick_kernel,
        out_shape=[out] * 8,
        in_specs=[smem] * 3 + [pl.BlockSpec(memory_space=pl.ANY)] * 8,
        out_specs=[pl.BlockSpec(memory_space=pltpu.VMEM)] * 8,
        scratch_shapes=[pltpu.SemaphoreType.DMA((16,))],
        name="pick_items",
    )(meta, slot, segment, *bufs)


def ring_rows(raw_x, raw_y):
    return [
        raw_x, pull(raw_x, 1, 0), pull(raw_x, 2, 0), pull(raw_x, -1, 0),
        raw_y, pull(raw_y, 0, 1), pull(raw_y, 0, 2), pull(raw_y, 0, -1),
    ]


def hand_over(items):
    return [
        items[0], pull(items[3], 0, 1), pull(items[2], 0, 2), pull(items[1], 0, -1),
        items[4], pull(items[7], 1, 0), pull(items[6], 2, 0), pull(items[5], -1, 0),
    ]


def keep_items(meta_ref, slot_ref, segment_ref, got, store):
    me = meta_ref[0]
    for f, along_x in enumerate((True, False)):
        _, across = place(me, along_x)
        for k in range(2):
            row = stored_row(slot_ref, segment_ref, me + k)
            _, owner_across = place(row // 4, along_x)
            source = lax.rem(owner_across - across + SIDE, SIDE)
            for d in range(SIDE):
                @pl.when(source == d)
                def _():
                    store(k, f * (RANK // 2), got[f * 4 + d][k])


def rank_kernel(meta_ref, slot_ref, segment_ref, tokens_ref, *refs):
    got, out_ref, down, swapped = refs[0:8], refs[8], refs[9], refs[10]

    def store(k, offset, block):
        part = block[:RANK // 2]
        down[k * RANK + offset:k * RANK + offset + RANK // 2, :] = part
        other = (1 - k) * RANK + offset
        swapped[other:other + RANK // 2, :] = part

    keep_items(meta_ref, slot_ref, segment_ref, got, store)
    cut = meta_ref[1]
    half = out_ref.shape[0]
    dims = (((1,), (1,)), ((), ()))
    tokens = tokens_ref[...]
    straight = lax.dot_general(tokens, down[...], dims, preferred_element_type=jnp.float32)
    crossed = lax.dot_general(tokens, swapped[...], dims, preferred_element_type=jnp.float32)
    row = lax.broadcasted_iota(jnp.int32, (half, 2 * RANK), 0)
    lane = lax.broadcasted_iota(jnp.int32, (half, 2 * RANK), 1)
    top = jnp.where(row < cut, straight[:half], crossed[:half])
    bottom = jnp.where(row + half < cut, crossed[half:], straight[half:])
    out_ref[...] = jnp.where(lane < RANK, top, bottom).astype(jnp.bfloat16)


def rank_part(meta, slot, segment, tokens, got):
    smem = pl.BlockSpec(memory_space=pltpu.SMEM)
    vmem = pl.BlockSpec(memory_space=pltpu.VMEM)
    rows, width = tokens.shape
    return pl.pallas_call(
        rank_kernel,
        out_shape=jax.ShapeDtypeStruct((rows // 2, 2 * RANK), jnp.bfloat16),
        in_specs=[smem] * 3 + [vmem] * 9,
        out_specs=vmem,
        scratch_shapes=[pltpu.VMEM((2 * RANK, width), jnp.bfloat16)] * 2,
        name="rank_part",
    )(meta, slot, segment, tokens, *got)


def query_kernel(meta_ref, slot_ref, segment_ref, base_ref, *refs):
    parts, got, q_ref, up = refs[0:8], refs[8:16], refs[16], refs[17]

    def store(k, offset, block):
        for start in ((k * RANK), (3 - k) * RANK):
            up[start + offset:start + offset + RANK // 2, :] = block[RANK // 2:]

    keep_items(meta_ref, slot_ref, segment_ref, got, store)
    cut = meta_ref[1]
    total = functools.reduce(jnp.add, [p[...].astype(jnp.float32) for p in parts])
    half = total.shape[0]
    row = lax.broadcasted_iota(jnp.int32, (half, 2 * RANK), 0)
    lane = lax.broadcasted_iota(jnp.int32, (half, 2 * RANK), 1)
    left = lane < RANK
    zero = jnp.zeros_like(total)

    def masked(keep):
        return jnp.where(keep, total, zero).astype(jnp.bfloat16)

    first, second = row < cut, row + half < cut
    lhs = jnp.concatenate(
        [
            jnp.concatenate([masked(left & first), masked(left & ~first)], axis=1),
            jnp.concatenate([masked(~left & ~second), masked(~left & second)], axis=1),
        ],
        axis=0,
    )
    tiles = 2 * half // TILE
    for t in range(tiles):
        rows = slice(t * TILE, (t + 1) * TILE)
        lora = jnp.dot(lhs[rows], up[...], preferred_element_type=jnp.float32)
        q = (base_ref[rows, :].astype(jnp.float32) + adapter_scale * lora).astype(jnp.bfloat16)
        for h in range(HEADS):
            at = (t * HEADS + h) * TILE
            q_ref[at:at + TILE, :] = q[:, h * HEAD_SIZE:(h + 1) * HEAD_SIZE]
    mixed = jnp.minimum(cut // TILE, tiles - 1)
    q_ref[tiles * STEP_ROWS:(tiles + 1) * STEP_ROWS, :] = q_ref[
        pl.ds(pl.multiple_of(mixed * STEP_ROWS, STEP_ROWS), STEP_ROWS), :
    ]


def queries(meta, slot, segment, base, parts, got):
    smem = pl.BlockSpec(memory_space=pltpu.SMEM)
    vmem = pl.BlockSpec(memory_space=pltpu.VMEM)
    rows, width = base.shape
    return pl.pallas_call(
        query_kernel,
        out_shape=jax.ShapeDtypeStruct((rows * HEADS + STEP_ROWS, HEAD_SIZE), jnp.bfloat16),
        in_specs=[smem] * 3 + [vmem] * 17,
        out_specs=vmem,
        scratch_shapes=[pltpu.VMEM((4 * RANK, width), jnp.bfloat16)],
        compiler_params=pltpu.CompilerParams(vmem_limit_bytes=VMEM_LIMIT),
        name="queries",
    )(meta, slot, segment, base, *parts, *got)


def attend_kernel(blocks, *refs):
    meta_ref, q_ref, span_ref, prev_ref, cache_ref, out_ref = refs[:6]
    (k_sc, v_sc, count_sc, steps, m_sc, al_sc, s_even, s_odd,
     id_rows, id_vec, id_sc, id_sem, k_sem, v_sem) = refs[6:]
    rows_all = q_ref.shape[0] - STEP_ROWS
    tiles = rows_all // STEP_ROWS
    keys_step = GROUP * PAGE
    groups = k_sc.shape[0] // 2 // keys_step
    own_rows = cache_ref.shape[0] // blocks
    own_pages = (own_rows - 16) // (2 * PAGE)
    seg_a, cut, prev_cut = meta_ref[0], meta_ref[1], meta_ref[2]

    for d in range(blocks):
        pltpu.make_async_copy(
            cache_ref.at[pl.ds((d + 1) * own_rows - 16, 16)], id_rows.at[d], id_sem.at[d]
        ).start()

    def rows_at(start):
        return pl.ds(pl.multiple_of(start, STEP_ROWS), STEP_ROWS)

    def keys_at(g):
        return pl.ds(pl.multiple_of(g * keys_step, keys_step), keys_step)

    def score(i, s_ref):
        at = jnp.minimum(steps[2 * i], rows_all)
        s_ref[...] = lax.dot_general(
            q_ref[rows_at(at), :],
            k_sc[keys_at(steps[2 * i + 1]), :],
            (((1,), (1,)), ((), ())),
            preferred_element_type=jnp.float32,
        )

    def soften(i, s_ref):
        rows = rows_at(steps[2 * i])
        parts = [s_ref[:, j * 128:(j + 1) * 128] for j in range(GROUP)]
        peak = jnp.max(functools.reduce(jnp.maximum, parts), axis=1, keepdims=True) * LOG_SCALE
        old = m_sc[rows, :]
        new = jnp.maximum(old, peak)
        fade = jnp.exp2(old - new)
        weights = jnp.concatenate(
            [jnp.exp2(s * LOG_SCALE - new).astype(jnp.bfloat16) for s in parts], axis=1
        )
        added = jnp.dot(weights, v_sc[keys_at(steps[2 * i + 1]), :], preferred_element_type=jnp.float32)
        m_sc[rows, :] = new
        al_sc[rows, 0:128] = al_sc[rows, 0:128] * fade + added[:, 0:128]
        al_sc[rows, 128:256] = al_sc[rows, 128:256] * fade + added[:, 128:256]

    for d in range(blocks):
        pltpu.make_async_copy(
            cache_ref.at[pl.ds((d + 1) * own_rows - 16, 16)], id_rows.at[d], id_sem.at[d]
        ).wait()
    for d in range(blocks):
        id_vec[d:d + 1, :] = id_rows[d].astype(jnp.int32)[0:1, :]
    copy = pltpu.make_async_copy(id_vec, id_sc, id_sem.at[0])
    copy.start()
    copy.wait()

    count_sc[0] = 0
    count_sc[1] = 0

    def page_copies(d, page, slot):
        here = pl.ds(pl.multiple_of(slot * PAGE, PAGE), PAGE)
        at = pl.multiple_of(d * own_rows + page * PAGE, 16)
        keys = pltpu.make_async_copy(cache_ref.at[pl.ds(at, PAGE)], k_sc.at[here], k_sem)
        at = pl.multiple_of(d * own_rows + (own_pages + page) * PAGE, 16)
        values = pltpu.make_async_copy(
            cache_ref.at[pl.ds(at, PAGE)], v_sc.at[here, pl.ds(0, 128)], v_sem
        )
        return keys, values

    @pl.loop(0, blocks * own_pages)
    def _(i):
        d, page = i // own_pages, lax.rem(i, own_pages)
        which = id_sc[d, page] - seg_a

        @pl.when((which == 0) | (which == 1))
        def _():
            n = count_sc[which]
            for c in page_copies(d, page, which * groups * GROUP + n):
                c.start()
            count_sc[which] = n + 1

    span_keys = jnp.concatenate([prev_ref[0:256, :], span_ref[0:256, :]], axis=0)
    span_values = jnp.concatenate(
        [
            jnp.concatenate([prev_ref[256:512, :], span_ref[256:512, :]], axis=0),
            jnp.ones((512, 128), jnp.bfloat16),
        ],
        axis=1,
    )

    @pl.loop(0, tiles)
    def _(t):
        rows = rows_at(t * STEP_ROWS)
        scores = lax.dot_general(
            q_ref[rows, :], span_keys, (((1,), (1,)), ((), ())), preferred_element_type=jnp.float32
        )
        token = t * TILE + lax.broadcasted_iota(jnp.int32, (STEP_ROWS, 512), 0) % TILE
        key = lax.broadcasted_iota(jnp.int32, (STEP_ROWS, 512), 1) - 256
        in_a = token < cut
        keep = ((key < 0) & in_a & (key + 256 >= prev_cut)) | (
            (key >= 0) & (key <= token) & ((key < cut) == in_a)
        )
        scores = jnp.where(keep, scores * LOG_SCALE, NEG)
        peak = jnp.max(scores, axis=1, keepdims=True)
        weights = jnp.exp2(scores - peak).astype(jnp.bfloat16)
        m_sc[rows, :] = jnp.broadcast_to(peak, (STEP_ROWS, 128))
        al_sc[rows, :] = jnp.dot(weights, span_values, preferred_element_type=jnp.float32)

    mixed_start = jnp.minimum(cut // TILE, tiles - 1) * STEP_ROWS
    mixed = rows_at(mixed_start)
    m_sc[rows_all:rows_all + STEP_ROWS, :] = m_sc[mixed, :]
    al_sc[rows_all:rows_all + STEP_ROWS, :] = al_sc[mixed, :]

    @pl.loop(0, count_sc[0] + count_sc[1])
    def _(i):
        for c in page_copies(0, 0, 0):
            c.wait()

    count_sc[2] = 0
    for side in range(2):
        n = count_sc[side]
        full = (n + GROUP - 1) // GROUP
        base = side * groups * keys_step

        @pl.loop(0, n)
        def _(i, base=base):
            there = pl.ds(pl.multiple_of(base + i * PAGE, PAGE), PAGE)
            v_sc[there, 128:256] = jnp.ones((PAGE, 128), jnp.bfloat16)

        @pl.loop(n, full * GROUP)
        def _(i, base=base):
            there = pl.ds(pl.multiple_of(base + i * PAGE, PAGE), PAGE)
            k_sc[there, :] = k_sc[base:base + PAGE, :]
            v_sc[there, :] = jnp.zeros((PAGE, 256), jnp.bfloat16)

        low = 0 if side == 0 else cut // TILE
        high = (cut + TILE - 1) // TILE if side == 0 else tiles

        @pl.loop(0, full)
        def _(g, side=side, low=low, high=high):
            @pl.loop(low, high)
            def _(t):
                c = count_sc[2]
                start = t * STEP_ROWS
                if side == 1:
                    start = jnp.where(t == low, rows_all, start)
                steps[2 * c] = start
                steps[2 * c + 1] = side * groups + g
                count_sc[2] = c + 1

    total = count_sc[2]
    for e in range(2):
        steps[2 * (total + e)] = rows_all + STEP_ROWS
        steps[2 * (total + e) + 1] = 0

    @pl.when(total > 0)
    def _():
        score(0, s_even)

    @pl.loop(0, (total + 1) // 2)
    def _(j):
        score(2 * j + 1, s_odd)
        soften(2 * j, s_even)
        score(2 * j + 2, s_even)
        soften(2 * j + 1, s_odd)

    token = (mixed_start // STEP_ROWS) * TILE + (
        lax.broadcasted_iota(jnp.int32, (STEP_ROWS, 128), 0) % TILE
    )
    in_a = token < cut
    for c in range(2):
        cols = slice(c * 128, (c + 1) * 128)
        al_sc[mixed, cols] = jnp.where(
            in_a, al_sc[mixed, cols], al_sc[rows_all:rows_all + STEP_ROWS, cols]
        )
    for t in range(tiles):
        for h in range(HEADS):
            at = (t * HEADS + h) * TILE
            out = al_sc[at:at + TILE, 0:128] / al_sc[at:at + TILE, 128:256]
            out_ref[t * TILE:(t + 1) * TILE, h * 128:(h + 1) * 128] = out.astype(jnp.bfloat16)


def attend(meta, q, span, prev, cache, blocks):
    rows = q.shape[0] - STEP_ROWS
    tiles = rows // STEP_ROWS
    pages = (cache.shape[0] // blocks - 16) // (2 * PAGE) * blocks
    groups = -(-pages // GROUP)
    vmem = pl.BlockSpec(memory_space=pltpu.VMEM)
    id_shape = (-(-blocks // 8) * 8, 128)
    return pl.pallas_call(
        functools.partial(attend_kernel, blocks),
        out_shape=jax.ShapeDtypeStruct((rows // HEADS, HEADS * HEAD_SIZE), jnp.bfloat16),
        in_specs=[pl.BlockSpec(memory_space=pltpu.SMEM), vmem, vmem, vmem, pl.BlockSpec(memory_space=pl.ANY)],
        out_specs=vmem,
        scratch_shapes=[
            pltpu.VMEM((2 * groups * GROUP * PAGE, 128), jnp.bfloat16),
            pltpu.VMEM((2 * groups * GROUP * PAGE, 256), jnp.bfloat16),
            pltpu.SMEM((3,), jnp.int32),
            pltpu.SMEM((2 * ((tiles + 1) * groups + 4),), jnp.int32),
            pltpu.VMEM((rows + 2 * STEP_ROWS, 128), jnp.float32),
            pltpu.VMEM((rows + 2 * STEP_ROWS, 256), jnp.float32),
            pltpu.VMEM((STEP_ROWS, GROUP * PAGE), jnp.float32),
            pltpu.VMEM((STEP_ROWS, GROUP * PAGE), jnp.float32),
            pltpu.VMEM((blocks, 16, 128), jnp.bfloat16),
            pltpu.VMEM(id_shape, jnp.int32),
            pltpu.SMEM(id_shape, jnp.int32),
            pltpu.SemaphoreType.DMA((blocks,)),
            pltpu.SemaphoreType.DMA(()),
            pltpu.SemaphoreType.DMA(()),
        ],
        compiler_params=pltpu.CompilerParams(vmem_limit_bytes=VMEM_LIMIT),
        name="attend",
    )(meta, q, span, prev, cache)


def per_device(
    tokens_in,
    base_queries,
    fresh_keys,
    fresh_values,
    cached_key_rows,
    cached_value_rows,
    adapter_store,
    adapter_slot,
    segment_adapter,
    token_request,
    cache_doc,
):
    tok_rows = tokens_in.shape[0]
    me = lax.axis_index("ctx")
    seg_a = token_request[0]
    cut = jnp.sum((token_request == seg_a).astype(jnp.int32))
    meta = jnp.stack([seg_a, cut])
    ids = (meta, adapter_slot, segment_adapter)

    docs = jnp.pad(cache_doc, (0, 128 - cache_doc.shape[0])).astype(jnp.bfloat16)
    own = jnp.concatenate(
        [cached_key_rows, cached_value_rows, jnp.broadcast_to(docs[None], (16, 128))], axis=0
    )
    cache = lax.all_gather(own, "ctx", axis=0, tiled=True)

    mid = RANK // 2
    width = adapter_store.shape[3]
    rows = ring_rows(
        adapter_store[:, :, :mid].reshape(-1, RANK, width),
        adapter_store[:, :, mid:].reshape(-1, RANK, width),
    )
    got = hand_over(pick(*ids, rows))

    span = jnp.concatenate(
        [fresh_keys, fresh_values, jnp.broadcast_to(cut.astype(jnp.bfloat16), (16, 128))], axis=0
    )
    prev = lax.ppermute(span, "ctx", [(i - 1, i) for i in range(1, SIDE * SIDE)])
    prev_cut = jnp.where(me == 0, tok_rows, prev[512, 0].astype(jnp.int32))

    acts = rank_part(*ids, tokens_in, got)
    parts = [acts] + [pull_tp(acts, dz, dc) for dz in range(SIDE) for dc in range(2) if dz or dc]
    query = queries(*ids, base_queries, parts, got)
    info = jnp.concatenate([meta, prev_cut[None]])
    return attend(info, query, span, prev, cache, SIDE * SIDE)


def solution(mesh):
    in_specs = (
        P("ctx", "tp"),
        P("ctx", "tp"),
        P("ctx", "tp"),
        P("ctx", "tp"),
        P("ctx", "tp"),
        P("ctx", "tp"),
        P("ctx", None, None, "tp"),
        P(),
        P(),
        P("ctx"),
        P("ctx"),
    )
    out_specs = P("ctx", "tp")
    return jax.shard_map(
        per_device, mesh=mesh, in_specs=in_specs, out_specs=out_specs, check_vma=False
    )
```

```python
import functools
import math

import jax
import jax.numpy as jnp
from jax import lax
from jax.experimental import pallas as pl
from jax.experimental.pallas import tpu as pltpu
from jax.sharding import PartitionSpec as P

HEAD_SIZE = 128
PAGE = 128
SIDE = 4
RANK = 64
HEADS = 8
TILE = 64
GROUP = 8
STEP_ROWS = TILE * HEADS
NEG = -1e30
VMEM_LIMIT = 56 * 1024 * 1024
LOG_SCALE = math.log2(math.e) / math.sqrt(HEAD_SIZE)

adapter_scale = 2.0


def pull(block, dx, dy):
    route = []
    for i in range(SIDE * SIDE):
        y, x = divmod(i, SIDE)
        route.append((((y + dy) % SIDE) * SIDE + (x + dx) % SIDE, i))
    return lax.ppermute(block, "ctx", route)


def pull_tp(block, dz, dc):
    route = []
    for i in range(2 * SIDE):
        z, c = divmod(i, 2)
        route.append((((z + dz) % SIDE) * 2 + (c ^ dc), i))
    return lax.ppermute(block, "tp", route)


def stored_row(slot_ref, segment_ref, segment):
    return slot_ref[segment_ref[segment]]


def place(index, along_x):
    y, x = index // SIDE, lax.rem(index, SIDE)
    return (x, y) if along_x else (y, x)


def pick_kernel(meta_ref, slot_ref, segment_ref, *refs):
    bufs, outs, sems = refs[0:10], refs[10:18], refs[18]
    me = meta_ref[0]
    for f, along_x in enumerate((True, False)):
        along, across = place(me, along_x)
        for d in range(SIDE):
            there = lax.rem(across + d, SIDE)
            dest = there * SIDE + along if along_x else along * SIDE + there
            for k in range(2):
                row = stored_row(slot_ref, segment_ref, dest + k)
                owner_along, _ = place(row // 4, along_x)
                ring = lax.rem(owner_along - along + SIDE, SIDE)
                index = lax.rem(row, 4)
                cases = (
                    (ring == 0, index),
                    (ring == 1, index),
                    (ring == 3, index),
                    ((ring == 2) & (index < 2), index),
                    ((ring == 2) & (index >= 2), index - 2),
                )
                for b, (found, at) in enumerate(cases):
                    @pl.when(found)
                    def _():
                        pltpu.make_async_copy(
                            bufs[f * 5 + b].at[at],
                            outs[f * 4 + d].at[k],
                            sems.at[f * 8 + d * 2 + k],
                        ).start()
    for f in range(2):
        for d in range(SIDE):
            for k in range(2):
                pltpu.make_async_copy(
                    bufs[f * 5].at[0], outs[f * 4 + d].at[k], sems.at[f * 8 + d * 2 + k]
                ).wait()


def pick(meta, slot, segment, bufs):
    out = jax.ShapeDtypeStruct((2,) + bufs[0].shape[1:], jnp.bfloat16)
    smem = pl.BlockSpec(memory_space=pltpu.SMEM)
    return pl.pallas_call(
        pick_kernel,
        out_shape=[out] * 8,
        in_specs=[smem] * 3 + [pl.BlockSpec(memory_space=pl.ANY)] * 10,
        out_specs=[pl.BlockSpec(memory_space=pltpu.VMEM)] * 8,
        scratch_shapes=[pltpu.SemaphoreType.DMA((16,))],
        name="pick_items",
    )(meta, slot, segment, *bufs)


def ring_rows(raw_x, raw_y):
    after_x, before_x = pull(raw_x, 1, 0), pull(raw_x, -1, 0)
    after_y, before_y = pull(raw_y, 0, 1), pull(raw_y, 0, -1)
    half = raw_x.shape[0] // 2
    return [
        raw_x, after_x, before_x, pull(after_x[:half], 1, 0), pull(before_x[half:], -1, 0),
        raw_y, after_y, before_y, pull(after_y[:half], 0, 1), pull(before_y[half:], 0, -1),
    ]


def hand_over(items):
    return [
        items[0], pull(items[3], 0, 1), pull(items[2], 0, 2), pull(items[1], 0, -1),
        items[4], pull(items[7], 1, 0), pull(items[6], 2, 0), pull(items[5], -1, 0),
    ]


def keep_items(meta_ref, slot_ref, segment_ref, got, store):
    me = meta_ref[0]
    for f, along_x in enumerate((True, False)):
        _, across = place(me, along_x)
        for k in range(2):
            row = stored_row(slot_ref, segment_ref, me + k)
            _, owner_across = place(row // 4, along_x)
            source = lax.rem(owner_across - across + SIDE, SIDE)
            for d in range(SIDE):
                @pl.when(source == d)
                def _():
                    store(k, f * (RANK // 2), got[f * 4 + d][k])


def rank_kernel(meta_ref, slot_ref, segment_ref, tokens_ref, *refs):
    got, out_ref, down, swapped = refs[0:8], refs[8], refs[9], refs[10]

    def store(k, offset, block):
        part = block[:RANK // 2]
        down[k * RANK + offset:k * RANK + offset + RANK // 2, :] = part
        other = (1 - k) * RANK + offset
        swapped[other:other + RANK // 2, :] = part

    keep_items(meta_ref, slot_ref, segment_ref, got, store)
    cut = meta_ref[1]
    half = out_ref.shape[0]
    dims = (((1,), (1,)), ((), ()))
    tokens = tokens_ref[...]
    straight = lax.dot_general(tokens, down[...], dims, preferred_element_type=jnp.float32)
    crossed = lax.dot_general(tokens, swapped[...], dims, preferred_element_type=jnp.float32)
    row = lax.broadcasted_iota(jnp.int32, (half, 2 * RANK), 0)
    lane = lax.broadcasted_iota(jnp.int32, (half, 2 * RANK), 1)
    top = jnp.where(row < cut, straight[:half], crossed[:half])
    bottom = jnp.where(row + half < cut, crossed[half:], straight[half:])
    out_ref[...] = jnp.where(lane < RANK, top, bottom).astype(jnp.bfloat16)


def rank_part(meta, slot, segment, tokens, got):
    smem = pl.BlockSpec(memory_space=pltpu.SMEM)
    vmem = pl.BlockSpec(memory_space=pltpu.VMEM)
    rows, width = tokens.shape
    return pl.pallas_call(
        rank_kernel,
        out_shape=jax.ShapeDtypeStruct((rows // 2, 2 * RANK), jnp.bfloat16),
        in_specs=[smem] * 3 + [vmem] * 9,
        out_specs=vmem,
        scratch_shapes=[pltpu.VMEM((2 * RANK, width), jnp.bfloat16)] * 2,
        name="rank_part",
    )(meta, slot, segment, tokens, *got)


def query_kernel(meta_ref, slot_ref, segment_ref, base_ref, *refs):
    parts, got, q_ref, up = refs[0:4], refs[4:12], refs[12], refs[13]

    def store(k, offset, block):
        for start in ((k * RANK), (3 - k) * RANK):
            up[start + offset:start + offset + RANK // 2, :] = block[RANK // 2:]

    keep_items(meta_ref, slot_ref, segment_ref, got, store)
    cut = meta_ref[1]
    total = functools.reduce(jnp.add, [p[...].astype(jnp.float32) for p in parts])
    half = total.shape[0]
    row = lax.broadcasted_iota(jnp.int32, (half, 2 * RANK), 0)
    lane = lax.broadcasted_iota(jnp.int32, (half, 2 * RANK), 1)
    left = lane < RANK
    zero = jnp.zeros_like(total)

    def masked(keep):
        return jnp.where(keep, total, zero).astype(jnp.bfloat16)

    first, second = row < cut, row + half < cut
    lhs = jnp.concatenate(
        [
            jnp.concatenate([masked(left & first), masked(left & ~first)], axis=1),
            jnp.concatenate([masked(~left & ~second), masked(~left & second)], axis=1),
        ],
        axis=0,
    )
    tiles = 2 * half // TILE
    for t in range(tiles):
        rows = slice(t * TILE, (t + 1) * TILE)
        lora = jnp.dot(lhs[rows], up[...], preferred_element_type=jnp.float32)
        q = (base_ref[rows, :].astype(jnp.float32) + adapter_scale * lora).astype(jnp.bfloat16)
        for h in range(HEADS):
            at = (t * HEADS + h) * TILE
            q_ref[at:at + TILE, :] = q[:, h * HEAD_SIZE:(h + 1) * HEAD_SIZE]
    mixed = jnp.minimum(cut // TILE, tiles - 1)
    q_ref[tiles * STEP_ROWS:(tiles + 1) * STEP_ROWS, :] = q_ref[
        pl.ds(pl.multiple_of(mixed * STEP_ROWS, STEP_ROWS), STEP_ROWS), :
    ]


def queries(meta, slot, segment, base, parts, got):
    smem = pl.BlockSpec(memory_space=pltpu.SMEM)
    vmem = pl.BlockSpec(memory_space=pltpu.VMEM)
    rows, width = base.shape
    return pl.pallas_call(
        query_kernel,
        out_shape=jax.ShapeDtypeStruct((rows * HEADS + STEP_ROWS, HEAD_SIZE), jnp.bfloat16),
        in_specs=[smem] * 3 + [vmem] * 13,
        out_specs=vmem,
        scratch_shapes=[pltpu.VMEM((4 * RANK, width), jnp.bfloat16)],
        compiler_params=pltpu.CompilerParams(vmem_limit_bytes=VMEM_LIMIT),
        name="queries",
    )(meta, slot, segment, base, *parts, *got)


def attend_kernel(blocks, *refs):
    meta_ref, q_ref, span_ref, prev_ref, cache_ref, out_ref = refs[:6]
    (k_sc, v_sc, count_sc, steps, m_sc, al_sc, s_even, s_odd,
     id_rows, id_vec, id_sc, id_sem, k_sem, v_sem) = refs[6:]
    rows_all = q_ref.shape[0] - STEP_ROWS
    tiles = rows_all // STEP_ROWS
    keys_step = GROUP * PAGE
    groups = k_sc.shape[0] // 2 // keys_step
    own_rows = cache_ref.shape[0] // blocks
    own_pages = (own_rows - 16) // (2 * PAGE)
    seg_a, cut = meta_ref[0], meta_ref[1]

    for d in range(blocks):
        pltpu.make_async_copy(
            cache_ref.at[pl.ds((d + 1) * own_rows - 16, 16)], id_rows.at[d], id_sem.at[d]
        ).start()

    def rows_at(start):
        return pl.ds(pl.multiple_of(start, STEP_ROWS), STEP_ROWS)

    def keys_at(g):
        return pl.ds(pl.multiple_of(g * keys_step, keys_step), keys_step)

    def score(i, s_ref):
        at = jnp.minimum(steps[2 * i], rows_all)
        s_ref[...] = lax.dot_general(
            q_ref[rows_at(at), :],
            k_sc[keys_at(steps[2 * i + 1]), :],
            (((1,), (1,)), ((), ())),
            preferred_element_type=jnp.float32,
        )

    def soften(i, s_ref):
        rows = rows_at(steps[2 * i])
        parts = [s_ref[:, j * 128:(j + 1) * 128] for j in range(GROUP)]
        peak = jnp.max(functools.reduce(jnp.maximum, parts), axis=1, keepdims=True) * LOG_SCALE
        old = m_sc[rows, :]
        new = jnp.maximum(old, peak)
        fade = jnp.exp2(old - new)
        weights = jnp.concatenate(
            [jnp.exp2(s * LOG_SCALE - new).astype(jnp.bfloat16) for s in parts], axis=1
        )
        added = jnp.dot(weights, v_sc[keys_at(steps[2 * i + 1]), :], preferred_element_type=jnp.float32)
        m_sc[rows, :] = new
        al_sc[rows, 0:128] = al_sc[rows, 0:128] * fade + added[:, 0:128]
        al_sc[rows, 128:256] = al_sc[rows, 128:256] * fade + added[:, 128:256]

    span_keys = jnp.concatenate([prev_ref[0:256, :], span_ref[0:256, :]], axis=0)
    span_values = jnp.concatenate(
        [
            jnp.concatenate([prev_ref[256:512, :], span_ref[256:512, :]], axis=0),
            jnp.ones((512, 128), jnp.bfloat16),
        ],
        axis=1,
    )

    before = jnp.max(prev_ref[512:528, :].astype(jnp.float32)).astype(jnp.int32)
    prev_cut = jnp.where(seg_a == 0, 256, before)

    def span_tile(t):
        rows = rows_at(t * STEP_ROWS)
        scores = lax.dot_general(
            q_ref[rows, :], span_keys, (((1,), (1,)), ((), ())), preferred_element_type=jnp.float32
        )
        token = t * TILE + lax.broadcasted_iota(jnp.int32, (STEP_ROWS, 512), 0) % TILE
        key = lax.broadcasted_iota(jnp.int32, (STEP_ROWS, 512), 1) - 256
        in_a = token < cut
        keep = ((key < 0) & in_a & (key + 256 >= prev_cut)) | (
            (key >= 0) & (key <= token) & ((key < cut) == in_a)
        )
        scores = jnp.where(keep, scores * LOG_SCALE, NEG)
        peak = jnp.max(scores, axis=1, keepdims=True)
        weights = jnp.exp2(scores - peak).astype(jnp.bfloat16)
        m_sc[rows, :] = jnp.broadcast_to(peak, (STEP_ROWS, 128))
        al_sc[rows, :] = jnp.dot(weights, span_values, preferred_element_type=jnp.float32)

    span_tile(0)
    for d in range(blocks):
        pltpu.make_async_copy(
            cache_ref.at[pl.ds((d + 1) * own_rows - 16, 16)], id_rows.at[d], id_sem.at[d]
        ).wait()
    for d in range(blocks):
        id_vec[d:d + 1, :] = id_rows[d].astype(jnp.int32)[0:1, :]
    copy = pltpu.make_async_copy(id_vec, id_sc, id_sem.at[0])
    copy.start()
    span_tile(1)
    copy.wait()

    count_sc[0] = 0
    count_sc[1] = 0

    def page_copies(d, page, slot):
        here = pl.ds(pl.multiple_of(slot * PAGE, PAGE), PAGE)
        at = pl.multiple_of(d * own_rows + page * PAGE, 16)
        keys = pltpu.make_async_copy(cache_ref.at[pl.ds(at, PAGE)], k_sc.at[here], k_sem)
        at = pl.multiple_of(d * own_rows + (own_pages + page) * PAGE, 16)
        values = pltpu.make_async_copy(
            cache_ref.at[pl.ds(at, PAGE)], v_sc.at[here, pl.ds(0, 128)], v_sem
        )
        return keys, values

    @pl.loop(0, blocks * own_pages)
    def _(i):
        d, page = i // own_pages, lax.rem(i, own_pages)
        which = id_sc[d, page] - seg_a

        @pl.when((which == 0) | (which == 1))
        def _():
            n = count_sc[which]
            for c in page_copies(d, page, which * groups * GROUP + n):
                c.start()
            count_sc[which] = n + 1

    for t in range(2, tiles):
        span_tile(t)

    mixed_start = jnp.minimum(cut // TILE, tiles - 1) * STEP_ROWS
    mixed = rows_at(mixed_start)
    m_sc[rows_all:rows_all + STEP_ROWS, :] = m_sc[mixed, :]
    al_sc[rows_all:rows_all + STEP_ROWS, :] = al_sc[mixed, :]

    @pl.loop(0, count_sc[0] + count_sc[1])
    def _(i):
        for c in page_copies(0, 0, 0):
            c.wait()

    count_sc[2] = 0
    for side in range(2):
        n = count_sc[side]
        full = (n + GROUP - 1) // GROUP
        base = side * groups * keys_step

        @pl.loop(0, n)
        def _(i, base=base):
            there = pl.ds(pl.multiple_of(base + i * PAGE, PAGE), PAGE)
            v_sc[there, 128:256] = jnp.ones((PAGE, 128), jnp.bfloat16)

        @pl.loop(n, full * GROUP)
        def _(i, base=base):
            there = pl.ds(pl.multiple_of(base + i * PAGE, PAGE), PAGE)
            k_sc[there, :] = k_sc[base:base + PAGE, :]
            v_sc[there, :] = jnp.zeros((PAGE, 256), jnp.bfloat16)

        low = 0 if side == 0 else cut // TILE
        high = (cut + TILE - 1) // TILE if side == 0 else tiles

        @pl.loop(0, full)
        def _(g, side=side, low=low, high=high):
            @pl.loop(low, high)
            def _(t):
                c = count_sc[2]
                start = t * STEP_ROWS
                if side == 1:
                    start = jnp.where(t == low, rows_all, start)
                steps[2 * c] = start
                steps[2 * c + 1] = side * groups + g
                count_sc[2] = c + 1

    total = count_sc[2]
    for e in range(2):
        steps[2 * (total + e)] = rows_all + STEP_ROWS
        steps[2 * (total + e) + 1] = 0

    @pl.when(total > 0)
    def _():
        score(0, s_even)

    @pl.loop(0, (total + 1) // 2)
    def _(j):
        score(2 * j + 1, s_odd)
        soften(2 * j, s_even)
        score(2 * j + 2, s_even)
        soften(2 * j + 1, s_odd)

    token = (mixed_start // STEP_ROWS) * TILE + (
        lax.broadcasted_iota(jnp.int32, (STEP_ROWS, 128), 0) % TILE
    )
    in_a = token < cut
    for c in range(2):
        cols = slice(c * 128, (c + 1) * 128)
        al_sc[mixed, cols] = jnp.where(
            in_a, al_sc[mixed, cols], al_sc[rows_all:rows_all + STEP_ROWS, cols]
        )
    for t in range(tiles):
        for h in range(HEADS):
            at = (t * HEADS + h) * TILE
            out = al_sc[at:at + TILE, 0:128] / al_sc[at:at + TILE, 128:256]
            out_ref[t * TILE:(t + 1) * TILE, h * 128:(h + 1) * 128] = out.astype(jnp.bfloat16)


def attend(meta, q, span, prev, cache, blocks):
    rows = q.shape[0] - STEP_ROWS
    tiles = rows // STEP_ROWS
    pages = (cache.shape[0] // blocks - 16) // (2 * PAGE) * blocks
    groups = -(-pages // GROUP)
    vmem = pl.BlockSpec(memory_space=pltpu.VMEM)
    id_shape = (-(-blocks // 8) * 8, 128)
    return pl.pallas_call(
        functools.partial(attend_kernel, blocks),
        out_shape=jax.ShapeDtypeStruct((rows // HEADS, HEADS * HEAD_SIZE), jnp.bfloat16),
        in_specs=[pl.BlockSpec(memory_space=pltpu.SMEM), vmem, vmem, vmem, pl.BlockSpec(memory_space=pl.ANY)],
        out_specs=vmem,
        scratch_shapes=[
            pltpu.VMEM((2 * groups * GROUP * PAGE, 128), jnp.bfloat16),
            pltpu.VMEM((2 * groups * GROUP * PAGE, 256), jnp.bfloat16),
            pltpu.SMEM((3,), jnp.int32),
            pltpu.SMEM((2 * ((tiles + 1) * groups + 4),), jnp.int32),
            pltpu.VMEM((rows + 2 * STEP_ROWS, 128), jnp.float32),
            pltpu.VMEM((rows + 2 * STEP_ROWS, 256), jnp.float32),
            pltpu.VMEM((STEP_ROWS, GROUP * PAGE), jnp.float32),
            pltpu.VMEM((STEP_ROWS, GROUP * PAGE), jnp.float32),
            pltpu.VMEM((blocks, 16, 128), jnp.bfloat16),
            pltpu.VMEM(id_shape, jnp.int32),
            pltpu.SMEM(id_shape, jnp.int32),
            pltpu.SemaphoreType.DMA((blocks,)),
            pltpu.SemaphoreType.DMA(()),
            pltpu.SemaphoreType.DMA(()),
        ],
        compiler_params=pltpu.CompilerParams(vmem_limit_bytes=VMEM_LIMIT),
        name="attend",
    )(meta, q, span, prev, cache)


def per_device(
    tokens_in,
    base_queries,
    fresh_keys,
    fresh_values,
    cached_key_rows,
    cached_value_rows,
    adapter_store,
    adapter_slot,
    segment_adapter,
    token_request,
    cache_doc,
):
    seg_a = token_request[0]
    cut = jnp.sum((token_request == seg_a).astype(jnp.int32))
    meta = jnp.stack([seg_a, cut])
    ids = (meta, adapter_slot, segment_adapter)

    docs = jnp.pad(cache_doc, (0, 128 - cache_doc.shape[0])).astype(jnp.bfloat16)
    own = jnp.concatenate(
        [cached_key_rows, cached_value_rows, jnp.broadcast_to(docs[None], (16, 128))], axis=0
    )
    cache = lax.all_gather(own, "ctx", axis=0, tiled=True)

    mid = RANK // 2
    width = adapter_store.shape[3]
    rows = ring_rows(
        adapter_store[:, :, :mid].reshape(-1, RANK, width),
        adapter_store[:, :, mid:].reshape(-1, RANK, width),
    )
    got = hand_over(pick(*ids, rows))

    span = jnp.concatenate(
        [fresh_keys, fresh_values, jnp.broadcast_to(cut.astype(jnp.bfloat16), (16, 128))], axis=0
    )
    acts = rank_part(*ids, tokens_in, got)
    pair = pull_tp(acts, 0, 1)
    pair, span = lax.optimization_barrier((pair, span))
    prev = lax.ppermute(span, "ctx", [(i - 1, i) for i in range(1, SIDE * SIDE)])
    acts = (acts.astype(jnp.float32) + pair.astype(jnp.float32)).astype(jnp.bfloat16)
    parts = [acts] + [pull_tp(acts, dz, 0) for dz in (1, 2, 3)]
    query = queries(*ids, base_queries, parts, got)
    return attend(meta, query, span, prev, cache, SIDE * SIDE)


def solution(mesh):
    in_specs = (
        P("ctx", "tp"),
        P("ctx", "tp"),
        P("ctx", "tp"),
        P("ctx", "tp"),
        P("ctx", "tp"),
        P("ctx", "tp"),
        P("ctx", None, None, "tp"),
        P(),
        P(),
        P("ctx"),
        P("ctx"),
    )
    out_specs = P("ctx", "tp")
    return jax.shard_map(
        per_device, mesh=mesh, in_specs=in_specs, out_specs=out_specs, check_vma=False
    )
```

```python
import functools
import math

import jax
import jax.numpy as jnp
from jax import lax
from jax.experimental import pallas as pl
from jax.experimental.pallas import tpu as pltpu
from jax.sharding import PartitionSpec as P

HEAD_SIZE = 128
PAGE = 128
SIDE = 4
RANK = 64
HEADS = 8
TILE = 64
GROUP = 8
STEP_ROWS = TILE * HEADS
NEG = -1e30
VMEM_LIMIT = 56 * 1024 * 1024
LOG_SCALE = math.log2(math.e) / math.sqrt(HEAD_SIZE)

adapter_scale = 2.0


def pull(block, dx, dy):
    route = []
    for i in range(SIDE * SIDE):
        y, x = divmod(i, SIDE)
        route.append((((y + dy) % SIDE) * SIDE + (x + dx) % SIDE, i))
    return lax.ppermute(block, "ctx", route)


def pull_tp(block, dz, dc):
    route = []
    for i in range(2 * SIDE):
        z, c = divmod(i, 2)
        route.append((((z + dz) % SIDE) * 2 + (c ^ dc), i))
    return lax.ppermute(block, "tp", route)


def stored_row(slot_ref, segment_ref, segment):
    return slot_ref[segment_ref[segment]]


def place(index, along_x):
    y, x = index // SIDE, lax.rem(index, SIDE)
    return (x, y) if along_x else (y, x)


def pick_kernel(meta_ref, slot_ref, segment_ref, *refs):
    bufs, outs, sems, owners, owner_sems = refs[0:10], refs[10:18], refs[18], refs[19], refs[20]
    me = meta_ref[0]
    stored = 4 * RANK
    found_at = ((bufs[0], stored), (bufs[1], stored), (bufs[2], stored), (bufs[4], stored // 2))
    owner_copies = [
        pltpu.make_async_copy(buf.at[pl.ds(start, 16)], owners.at[n], owner_sems.at[n])
        for n, (buf, start) in enumerate(found_at)
    ]
    for c in owner_copies:
        c.start()
    for f, along_x in enumerate((True, False)):
        along, across = place(me, along_x)
        for d in range(SIDE):
            there = lax.rem(across + d, SIDE)
            dest = there * SIDE + along if along_x else along * SIDE + there
            for k in range(2):
                row = stored_row(slot_ref, segment_ref, dest + k)
                owner_along, _ = place(row // 4, along_x)
                ring = lax.rem(owner_along - along + SIDE, SIDE)
                index = lax.rem(row, 4)
                cases = (
                    (ring == 0, index),
                    (ring == 1, index),
                    (ring == 3, index),
                    ((ring == 2) & (index < 2), index),
                    ((ring == 2) & (index >= 2), index - 2),
                )
                for b, (found, at) in enumerate(cases):
                    @pl.when(found)
                    def _():
                        pltpu.make_async_copy(
                            bufs[f * 5 + b].at[pl.ds(pl.multiple_of(at * RANK, RANK), RANK)],
                            outs[f * 4 + d].at[pl.ds(k * RANK, RANK)],
                            sems.at[f * 8 + d * 2 + k],
                        ).start()
    for c in owner_copies:
        c.wait()
    total = functools.reduce(jnp.add, [owners[n].astype(jnp.float32) for n in range(SIDE)])
    for d in range(SIDE):
        outs[d][2 * RANK:, :] = total.astype(jnp.bfloat16)
    for f in range(2):
        for d in range(SIDE):
            for k in range(2):
                pltpu.make_async_copy(
                    bufs[f * 5].at[pl.ds(0, RANK)],
                    outs[f * 4 + d].at[pl.ds(k * RANK, RANK)],
                    sems.at[f * 8 + d * 2 + k],
                ).wait()


def pick(meta, slot, segment, bufs):
    width = bufs[0].shape[1]
    with_owners = jax.ShapeDtypeStruct((2 * RANK + 16, width), jnp.bfloat16)
    without = jax.ShapeDtypeStruct((2 * RANK, width), jnp.bfloat16)
    smem = pl.BlockSpec(memory_space=pltpu.SMEM)
    return pl.pallas_call(
        pick_kernel,
        out_shape=[with_owners] * 4 + [without] * 4,
        in_specs=[smem] * 3 + [pl.BlockSpec(memory_space=pl.ANY)] * 10,
        out_specs=[pl.BlockSpec(memory_space=pltpu.VMEM)] * 8,
        scratch_shapes=[
            pltpu.SemaphoreType.DMA((16,)),
            pltpu.VMEM((SIDE, 16, width), jnp.bfloat16),
            pltpu.SemaphoreType.DMA((SIDE,)),
        ],
        name="pick_items",
    )(meta, slot, segment, *bufs)


def ring_rows(raw_x, raw_y, span):
    after_x, before_x = pull(raw_x, 1, 0), pull(raw_x, -1, 0)
    after_y, before_y = pull(raw_y, 0, 1), pull(raw_y, 0, -1)
    prev = lax.ppermute(span, "ctx", [(i - 1, i) for i in range(1, SIDE * SIDE)])
    before_x, prev = lax.optimization_barrier((before_x, prev))
    half = raw_y.shape[0] // 2
    return [
        raw_x, after_x, before_x, pull(after_x[:half], 1, 0), pull(before_x[half:], -1, 0),
        raw_y, after_y, before_y, pull(after_y[:half], 0, 1), pull(before_y[half:], 0, -1),
    ], prev


def hand_over(items):
    return [
        items[0], pull(items[3], 0, 1), pull(items[2], 0, 2), pull(items[1], 0, -1),
        items[4], pull(items[7], 1, 0), pull(items[6], 2, 0), pull(items[5], -1, 0),
    ]


def keep_items(meta_ref, slot_ref, segment_ref, got, part, store):
    me = meta_ref[0]
    half = RANK // 2
    for f, along_x in enumerate((True, False)):
        _, across = place(me, along_x)
        for k in range(2):
            row = stored_row(slot_ref, segment_ref, me + k)
            _, owner_across = place(row // 4, along_x)
            source = lax.rem(owner_across - across + SIDE, SIDE)
            block = slice(k * RANK + part * half, k * RANK + (part + 1) * half)
            for d in range(SIDE):
                @pl.when(source == d)
                def _():
                    store(k, f * half, got[f * 4 + d][block, :])


def rank_kernel(meta_ref, slot_ref, segment_ref, tokens_ref, *refs):
    got, (out_ref, down, swapped) = refs[0:8], refs[8:]

    def store(k, rank, block):
        down[k * RANK + rank:k * RANK + rank + RANK // 2, :] = block
        other = (1 - k) * RANK + rank
        swapped[other:other + RANK // 2, :] = block

    keep_items(meta_ref, slot_ref, segment_ref, got, 0, store)
    cut = meta_ref[1]
    half = out_ref.shape[0]
    dims = (((1,), (1,)), ((), ()))
    tokens = tokens_ref[...]
    straight = lax.dot_general(tokens, down[...], dims, preferred_element_type=jnp.float32)
    crossed = lax.dot_general(tokens, swapped[...], dims, preferred_element_type=jnp.float32)
    row = lax.broadcasted_iota(jnp.int32, (half, 2 * RANK), 0)
    lane = lax.broadcasted_iota(jnp.int32, (half, 2 * RANK), 1)
    top = jnp.where(row < cut, straight[:half], crossed[:half])
    bottom = jnp.where(row + half < cut, crossed[half:], straight[half:])
    out_ref[...] = jnp.where(lane < RANK, top, bottom).astype(jnp.bfloat16)


def rank_part(meta, slot, segment, tokens, got):
    smem = pl.BlockSpec(memory_space=pltpu.SMEM)
    vmem = pl.BlockSpec(memory_space=pltpu.VMEM)
    rows, width = tokens.shape
    return pl.pallas_call(
        rank_kernel,
        out_shape=jax.ShapeDtypeStruct((rows // 2, 2 * RANK), jnp.bfloat16),
        in_specs=[smem] * 3 + [vmem] * 9,
        out_specs=vmem,
        scratch_shapes=[pltpu.VMEM((2 * RANK, width), jnp.bfloat16)] * 2,
        name="rank_part",
    )(meta, slot, segment, tokens, *got)


def query_kernel(meta_ref, slot_ref, segment_ref, base_ref, *refs):
    parts, got, (q_ref, up) = refs[0:4], refs[4:12], refs[12:]

    def store(k, rank, block):
        for start in (k * RANK + rank, (3 - k) * RANK + rank):
            up[start:start + RANK // 2, :] = block

    keep_items(meta_ref, slot_ref, segment_ref, got, 1, store)
    cut = meta_ref[1]
    total = functools.reduce(jnp.add, [p[...].astype(jnp.float32) for p in parts])
    half = total.shape[0]
    row = lax.broadcasted_iota(jnp.int32, (half, 2 * RANK), 0)
    lane = lax.broadcasted_iota(jnp.int32, (half, 2 * RANK), 1)
    left = lane < RANK
    zero = jnp.zeros_like(total)

    def masked(keep):
        return jnp.where(keep, total, zero).astype(jnp.bfloat16)

    first, second = row < cut, row + half < cut
    lhs = jnp.concatenate(
        [
            jnp.concatenate([masked(left & first), masked(left & ~first)], axis=1),
            jnp.concatenate([masked(~left & ~second), masked(~left & second)], axis=1),
        ],
        axis=0,
    )
    tiles = 2 * half // TILE
    for t in range(tiles):
        rows = slice(t * TILE, (t + 1) * TILE)
        lora = jnp.dot(lhs[rows], up[...], preferred_element_type=jnp.float32)
        q = (base_ref[rows, :].astype(jnp.float32) + adapter_scale * lora).astype(jnp.bfloat16)
        for h in range(HEADS):
            at = (t * HEADS + h) * TILE
            q_ref[at:at + TILE, :] = q[:, h * HEAD_SIZE:(h + 1) * HEAD_SIZE]
    mixed = jnp.minimum(cut // TILE, tiles - 1)
    q_ref[tiles * STEP_ROWS:(tiles + 1) * STEP_ROWS, :] = q_ref[
        pl.ds(pl.multiple_of(mixed * STEP_ROWS, STEP_ROWS), STEP_ROWS), :
    ]


def queries(meta, slot, segment, base, parts, got):
    smem = pl.BlockSpec(memory_space=pltpu.SMEM)
    vmem = pl.BlockSpec(memory_space=pltpu.VMEM)
    rows, width = base.shape
    return pl.pallas_call(
        query_kernel,
        out_shape=jax.ShapeDtypeStruct((rows * HEADS + STEP_ROWS, HEAD_SIZE), jnp.bfloat16),
        in_specs=[smem] * 3 + [vmem] * 13,
        out_specs=vmem,
        scratch_shapes=[
            pltpu.VMEM((4 * RANK, width), jnp.bfloat16),
        ],
        compiler_params=pltpu.CompilerParams(vmem_limit_bytes=VMEM_LIMIT),
        name="queries",
    )(meta, slot, segment, base, *parts, *got)


def attend_kernel(blocks, *refs):
    meta_ref, ids_ref, q_ref, span_ref, prev_ref, cache_ref, out_ref = refs[:7]
    k_sc, v_sc, count_sc, steps, m_sc, al_sc, s_even, s_odd, k_sem, v_sem = refs[7:]
    rows_all = q_ref.shape[0] - STEP_ROWS
    tiles = rows_all // STEP_ROWS
    keys_step = GROUP * PAGE
    groups = k_sc.shape[0] // 2 // keys_step
    own_rows = cache_ref.shape[0] // blocks
    own_pages = own_rows // (2 * PAGE)
    seg_a, cut = meta_ref[0], meta_ref[1]

    def rows_at(start):
        return pl.ds(pl.multiple_of(start, STEP_ROWS), STEP_ROWS)

    def keys_at(g):
        return pl.ds(pl.multiple_of(g * keys_step, keys_step), keys_step)

    def score(i, s_ref):
        at = jnp.minimum(steps[2 * i], rows_all)
        s_ref[...] = lax.dot_general(
            q_ref[rows_at(at), :],
            k_sc[keys_at(steps[2 * i + 1]), :],
            (((1,), (1,)), ((), ())),
            preferred_element_type=jnp.float32,
        )

    def soften(i, s_ref):
        rows = rows_at(steps[2 * i])
        parts = [s_ref[:, j * 128:(j + 1) * 128] for j in range(GROUP)]
        peak = jnp.max(functools.reduce(jnp.maximum, parts), axis=1, keepdims=True) * LOG_SCALE
        old = m_sc[rows, :]
        new = jnp.maximum(old, peak)
        fade = jnp.exp2(old - new)
        weights = jnp.concatenate(
            [jnp.exp2(s * LOG_SCALE - new).astype(jnp.bfloat16) for s in parts], axis=1
        )
        added = jnp.dot(weights, v_sc[keys_at(steps[2 * i + 1]), :], preferred_element_type=jnp.float32)
        m_sc[rows, :] = new
        al_sc[rows, 0:128] = al_sc[rows, 0:128] * fade + added[:, 0:128]
        al_sc[rows, 128:256] = al_sc[rows, 128:256] * fade + added[:, 128:256]

    span_keys = jnp.concatenate([prev_ref[0:256, :], span_ref[0:256, :]], axis=0)
    span_values = jnp.concatenate(
        [
            jnp.concatenate([prev_ref[256:512, :], span_ref[256:512, :]], axis=0),
            jnp.ones((512, 128), jnp.bfloat16),
        ],
        axis=1,
    )

    before = jnp.max(prev_ref[512:528, :].astype(jnp.float32)).astype(jnp.int32)
    prev_cut = jnp.where(seg_a == 0, 256, before)

    def span_tile(t):
        rows = rows_at(t * STEP_ROWS)
        scores = lax.dot_general(
            q_ref[rows, :], span_keys, (((1,), (1,)), ((), ())), preferred_element_type=jnp.float32
        )
        token = t * TILE + lax.broadcasted_iota(jnp.int32, (STEP_ROWS, 512), 0) % TILE
        key = lax.broadcasted_iota(jnp.int32, (STEP_ROWS, 512), 1) - 256
        in_a = token < cut
        keep = ((key < 0) & in_a & (key + 256 >= prev_cut)) | (
            (key >= 0) & (key <= token) & ((key < cut) == in_a)
        )
        scores = jnp.where(keep, scores * LOG_SCALE, NEG)
        peak = jnp.max(scores, axis=1, keepdims=True)
        weights = jnp.exp2(scores - peak).astype(jnp.bfloat16)
        m_sc[rows, :] = jnp.broadcast_to(peak, (STEP_ROWS, 128))
        al_sc[rows, :] = jnp.dot(weights, span_values, preferred_element_type=jnp.float32)

    count_sc[0] = 0
    count_sc[1] = 0

    def page_copies(d, page, slot):
        here = pl.ds(pl.multiple_of(slot * PAGE, PAGE), PAGE)
        at = pl.multiple_of(d * own_rows + page * PAGE, 16)
        keys = pltpu.make_async_copy(cache_ref.at[pl.ds(at, PAGE)], k_sc.at[here], k_sem)
        at = pl.multiple_of(d * own_rows + (own_pages + page) * PAGE, 16)
        values = pltpu.make_async_copy(
            cache_ref.at[pl.ds(at, PAGE)], v_sc.at[here, pl.ds(0, 128)], v_sem
        )
        return keys, values

    @pl.loop(0, blocks * own_pages)
    def _(i):
        d, page = i // own_pages, lax.rem(i, own_pages)
        which = ids_ref[i] - seg_a

        @pl.when((which == 0) | (which == 1))
        def _():
            n = count_sc[which]
            for c in page_copies(d, page, which * groups * GROUP + n):
                c.start()
            count_sc[which] = n + 1

    for t in range(tiles):
        span_tile(t)

    mixed_start = jnp.minimum(cut // TILE, tiles - 1) * STEP_ROWS
    mixed = rows_at(mixed_start)
    m_sc[rows_all:rows_all + STEP_ROWS, :] = m_sc[mixed, :]
    al_sc[rows_all:rows_all + STEP_ROWS, :] = al_sc[mixed, :]

    @pl.loop(0, count_sc[0] + count_sc[1])
    def _(i):
        for c in page_copies(0, 0, 0):
            c.wait()

    count_sc[2] = 0
    for side in range(2):
        n = count_sc[side]
        full = (n + GROUP - 1) // GROUP
        base = side * groups * keys_step

        @pl.loop(0, n)
        def _(i, base=base):
            there = pl.ds(pl.multiple_of(base + i * PAGE, PAGE), PAGE)
            v_sc[there, 128:256] = jnp.ones((PAGE, 128), jnp.bfloat16)

        @pl.loop(n, full * GROUP)
        def _(i, base=base):
            there = pl.ds(pl.multiple_of(base + i * PAGE, PAGE), PAGE)
            k_sc[there, :] = k_sc[base:base + PAGE, :]
            v_sc[there, :] = jnp.zeros((PAGE, 256), jnp.bfloat16)

        low = 0 if side == 0 else cut // TILE
        high = (cut + TILE - 1) // TILE if side == 0 else tiles

        @pl.loop(0, full)
        def _(g, side=side, low=low, high=high):
            @pl.loop(low, high)
            def _(t):
                c = count_sc[2]
                start = t * STEP_ROWS
                if side == 1:
                    start = jnp.where(t == low, rows_all, start)
                steps[2 * c] = start
                steps[2 * c + 1] = side * groups + g
                count_sc[2] = c + 1

    total = count_sc[2]
    for e in range(2):
        steps[2 * (total + e)] = rows_all + STEP_ROWS
        steps[2 * (total + e) + 1] = 0

    @pl.when(total > 0)
    def _():
        score(0, s_even)

    @pl.loop(0, (total + 1) // 2)
    def _(j):
        score(2 * j + 1, s_odd)
        soften(2 * j, s_even)
        score(2 * j + 2, s_even)
        soften(2 * j + 1, s_odd)

    token = (mixed_start // STEP_ROWS) * TILE + (
        lax.broadcasted_iota(jnp.int32, (STEP_ROWS, 128), 0) % TILE
    )
    in_a = token < cut
    for c in range(2):
        cols = slice(c * 128, (c + 1) * 128)
        al_sc[mixed, cols] = jnp.where(
            in_a, al_sc[mixed, cols], al_sc[rows_all:rows_all + STEP_ROWS, cols]
        )
    for t in range(tiles):
        for h in range(HEADS):
            at = (t * HEADS + h) * TILE
            out = al_sc[at:at + TILE, 0:128] / al_sc[at:at + TILE, 128:256]
            out_ref[t * TILE:(t + 1) * TILE, h * 128:(h + 1) * 128] = out.astype(jnp.bfloat16)


def attend(meta, ids, q, span, prev, cache, blocks):
    rows = q.shape[0] - STEP_ROWS
    tiles = rows // STEP_ROWS
    groups = -(-ids.shape[0] // GROUP)
    vmem = pl.BlockSpec(memory_space=pltpu.VMEM)
    return pl.pallas_call(
        functools.partial(attend_kernel, blocks),
        out_shape=jax.ShapeDtypeStruct((rows // HEADS, HEADS * HEAD_SIZE), jnp.bfloat16),
        in_specs=[pl.BlockSpec(memory_space=pltpu.SMEM)] * 2
        + [vmem] * 3
        + [pl.BlockSpec(memory_space=pl.ANY)],
        out_specs=vmem,
        scratch_shapes=[
            pltpu.VMEM((2 * groups * GROUP * PAGE, 128), jnp.bfloat16),
            pltpu.VMEM((2 * groups * GROUP * PAGE, 256), jnp.bfloat16),
            pltpu.SMEM((3,), jnp.int32),
            pltpu.SMEM((2 * ((tiles + 1) * groups + 4),), jnp.int32),
            pltpu.VMEM((rows + 2 * STEP_ROWS, 128), jnp.float32),
            pltpu.VMEM((rows + 2 * STEP_ROWS, 256), jnp.float32),
            pltpu.VMEM((STEP_ROWS, GROUP * PAGE), jnp.float32),
            pltpu.VMEM((STEP_ROWS, GROUP * PAGE), jnp.float32),
            pltpu.SemaphoreType.DMA(()),
            pltpu.SemaphoreType.DMA(()),
        ],
        compiler_params=pltpu.CompilerParams(vmem_limit_bytes=VMEM_LIMIT),
        name="attend",
    )(meta, ids, q, span, prev, cache)


def per_device(
    tokens_in,
    base_queries,
    fresh_keys,
    fresh_values,
    cached_key_rows,
    cached_value_rows,
    adapter_store,
    adapter_slot,
    segment_adapter,
    token_request,
    cache_doc,
):
    seg_a = token_request[0]
    cut = jnp.sum((token_request == seg_a).astype(jnp.int32))
    meta = jnp.stack([seg_a, cut])

    own = jnp.concatenate([cached_key_rows, cached_value_rows], axis=0)
    cache = lax.all_gather(own, "ctx", axis=0, tiled=True)

    mid = RANK // 2
    width = adapter_store.shape[3]
    pages = cache_doc.shape[0]
    lane = jnp.arange(width, dtype=jnp.int32)
    docs = jnp.tile(cache_doc, width // pages)
    docs = jnp.where(lane // pages == lax.axis_index("ctx"), docs, 0).astype(jnp.bfloat16)
    span = jnp.concatenate(
        [fresh_keys, fresh_values, jnp.broadcast_to(cut.astype(jnp.bfloat16), (16, 128))], axis=0
    )
    rows, prev = ring_rows(
        jnp.concatenate(
            [
                adapter_store[:, :, :mid].reshape(-1, width),
                jnp.broadcast_to(docs[None], (16, width)),
            ],
            axis=0,
        ),
        adapter_store[:, :, mid:].reshape(-1, width),
        span,
    )

    ids = (meta, adapter_slot, segment_adapter)
    got = hand_over(pick(*ids, rows))
    owners = functools.reduce(jnp.add, [g[2 * RANK, :SIDE * SIDE * pages].astype(jnp.int32) for g in got[:4]])

    acts = rank_part(*ids, tokens_in, got)
    pair = pull_tp(acts, 0, 1)
    acts = (acts.astype(jnp.float32) + pair.astype(jnp.float32)).astype(jnp.bfloat16)
    parts = [acts] + [pull_tp(acts, dz, 0) for dz in (1, 2, 3)]
    query = queries(*ids, base_queries, parts, got)
    return attend(meta, owners, query, span, prev, cache, SIDE * SIDE)


def solution(mesh):
    in_specs = (
        P("ctx", "tp"),
        P("ctx", "tp"),
        P("ctx", "tp"),
        P("ctx", "tp"),
        P("ctx", "tp"),
        P("ctx", "tp"),
        P("ctx", None, None, "tp"),
        P(),
        P(),
        P("ctx"),
        P("ctx"),
    )
    out_specs = P("ctx", "tp")
    return jax.shard_map(
        per_device, mesh=mesh, in_specs=in_specs, out_specs=out_specs, check_vma=False
    )
```

```python
import functools
import math

import jax
import jax.numpy as jnp
from jax import lax
from jax.experimental import pallas as pl
from jax.experimental.pallas import tpu as pltpu
from jax.sharding import PartitionSpec as P

HEAD_SIZE = 128
PAGE = 128
SIDE = 4
RANK = 64
HEADS = 8
TILE = 64
PART = TILE // 2
GROUP = 8
STEP_ROWS = TILE * HEADS
PART_ROWS = PART * HEADS
NEG = -1e30
LARGEST_SUM = 2.0**90
VMEM_LIMIT = 56 * 1024 * 1024
LOG_SCALE = math.log2(math.e) / math.sqrt(HEAD_SIZE)

adapter_scale = 2.0


def pull(block, dx, dy):
    route = []
    for i in range(SIDE * SIDE):
        y, x = divmod(i, SIDE)
        route.append((((y + dy) % SIDE) * SIDE + (x + dx) % SIDE, i))
    return lax.ppermute(block, "ctx", route)


def pull_tp(block, dz, dc):
    route = []
    for i in range(2 * SIDE):
        z, c = divmod(i, 2)
        route.append((((z + dz) % SIDE) * 2 + (c ^ dc), i))
    return lax.ppermute(block, "tp", route)


def stored_row(slot_ref, segment_ref, segment):
    return slot_ref[segment_ref[segment]]


def place(index, along_x):
    y, x = index // SIDE, lax.rem(index, SIDE)
    return (x, y) if along_x else (y, x)


def pick_kernel(meta_ref, slot_ref, segment_ref, *refs):
    bufs, outs, sems, owners, owner_sems = refs[0:10], refs[10:18], refs[18], refs[19], refs[20]
    me = meta_ref[0]
    stored = 4 * RANK
    found_at = ((bufs[0], stored), (bufs[1], stored), (bufs[2], stored), (bufs[4], stored // 2))
    owner_copies = [
        pltpu.make_async_copy(buf.at[pl.ds(start, 16)], owners.at[n], owner_sems.at[n])
        for n, (buf, start) in enumerate(found_at)
    ]
    for c in owner_copies:
        c.start()
    for f, along_x in enumerate((True, False)):
        along, across = place(me, along_x)
        for d in range(SIDE):
            there = lax.rem(across + d, SIDE)
            dest = there * SIDE + along if along_x else along * SIDE + there
            for k in range(2):
                row = stored_row(slot_ref, segment_ref, dest + k)
                owner_along, _ = place(row // 4, along_x)
                ring = lax.rem(owner_along - along + SIDE, SIDE)
                index = lax.rem(row, 4)
                cases = (
                    (ring == 0, index),
                    (ring == 1, index),
                    (ring == 3, index),
                    ((ring == 2) & (index < 2), index),
                    ((ring == 2) & (index >= 2), index - 2),
                )
                for b, (found, at) in enumerate(cases):
                    @pl.when(found)
                    def _():
                        pltpu.make_async_copy(
                            bufs[f * 5 + b].at[pl.ds(pl.multiple_of(at * RANK, RANK), RANK)],
                            outs[f * 4 + d].at[pl.ds(k * RANK, RANK)],
                            sems.at[f * 8 + d * 2 + k],
                        ).start()
    for c in owner_copies:
        c.wait()
    total = functools.reduce(jnp.add, [owners[n].astype(jnp.float32) for n in range(SIDE)])
    for d in range(SIDE):
        outs[d][2 * RANK:, :] = total.astype(jnp.bfloat16)
    for f in range(2):
        for d in range(SIDE):
            for k in range(2):
                pltpu.make_async_copy(
                    bufs[f * 5].at[pl.ds(0, RANK)],
                    outs[f * 4 + d].at[pl.ds(k * RANK, RANK)],
                    sems.at[f * 8 + d * 2 + k],
                ).wait()


def pick(meta, slot, segment, bufs):
    width = bufs[0].shape[1]
    with_owners = jax.ShapeDtypeStruct((2 * RANK + 16, width), jnp.bfloat16)
    without = jax.ShapeDtypeStruct((2 * RANK, width), jnp.bfloat16)
    smem = pl.BlockSpec(memory_space=pltpu.SMEM)
    return pl.pallas_call(
        pick_kernel,
        out_shape=[with_owners] * 4 + [without] * 4,
        in_specs=[smem] * 3 + [pl.BlockSpec(memory_space=pl.ANY)] * 10,
        out_specs=[pl.BlockSpec(memory_space=pltpu.VMEM)] * 8,
        scratch_shapes=[
            pltpu.SemaphoreType.DMA((16,)),
            pltpu.VMEM((SIDE, 16, width), jnp.bfloat16),
            pltpu.SemaphoreType.DMA((SIDE,)),
        ],
        name="pick_items",
    )(meta, slot, segment, *bufs)


def ring_rows(raw_x, raw_y, span):
    after_x, before_x = pull(raw_x, 1, 0), pull(raw_x, -1, 0)
    after_y, before_y = pull(raw_y, 0, 1), pull(raw_y, 0, -1)
    prev = lax.ppermute(span, "ctx", [(i - 1, i) for i in range(1, SIDE * SIDE)])
    before_x, prev = lax.optimization_barrier((before_x, prev))
    half = raw_y.shape[0] // 2
    return [
        raw_x, after_x, before_x, pull(after_x[:half], 1, 0), pull(before_x[half:], -1, 0),
        raw_y, after_y, before_y, pull(after_y[:half], 0, 1), pull(before_y[half:], 0, -1),
    ], prev


def hand_over(items):
    return [
        items[0], pull(items[3], 0, 1), pull(items[2], 0, 2), pull(items[1], 0, -1),
        items[4], pull(items[7], 1, 0), pull(items[6], 2, 0), pull(items[5], -1, 0),
    ]


def keep_items(meta_ref, slot_ref, segment_ref, got, part, store):
    me = meta_ref[0]
    half = RANK // 2
    for f, along_x in enumerate((True, False)):
        _, across = place(me, along_x)
        for k in range(2):
            row = stored_row(slot_ref, segment_ref, me + k)
            _, owner_across = place(row // 4, along_x)
            source = lax.rem(owner_across - across + SIDE, SIDE)
            block = slice(k * RANK + part * half, k * RANK + (part + 1) * half)
            for d in range(SIDE):
                @pl.when(source == d)
                def _():
                    store(k, f * half, got[f * 4 + d][block, :])


def rank_kernel(meta_ref, slot_ref, segment_ref, tokens_ref, *refs):
    got, (out_ref, down, swapped) = refs[0:8], refs[8:]

    def store(k, rank, block):
        down[k * RANK + rank:k * RANK + rank + RANK // 2, :] = block
        other = (1 - k) * RANK + rank
        swapped[other:other + RANK // 2, :] = block

    keep_items(meta_ref, slot_ref, segment_ref, got, 0, store)
    cut = meta_ref[1]
    half = out_ref.shape[0]
    dims = (((1,), (1,)), ((), ()))
    tokens = tokens_ref[...]
    straight = lax.dot_general(tokens, down[...], dims, preferred_element_type=jnp.float32)
    crossed = lax.dot_general(tokens, swapped[...], dims, preferred_element_type=jnp.float32)
    row = lax.broadcasted_iota(jnp.int32, (half, 2 * RANK), 0)
    lane = lax.broadcasted_iota(jnp.int32, (half, 2 * RANK), 1)
    top = jnp.where(row < cut, straight[:half], crossed[:half])
    bottom = jnp.where(row + half < cut, crossed[half:], straight[half:])
    out_ref[...] = jnp.where(lane < RANK, top, bottom).astype(jnp.bfloat16)


def rank_part(meta, slot, segment, tokens, got):
    smem = pl.BlockSpec(memory_space=pltpu.SMEM)
    vmem = pl.BlockSpec(memory_space=pltpu.VMEM)
    rows, width = tokens.shape
    return pl.pallas_call(
        rank_kernel,
        out_shape=jax.ShapeDtypeStruct((rows // 2, 2 * RANK), jnp.bfloat16),
        in_specs=[smem] * 3 + [vmem] * 9,
        out_specs=vmem,
        scratch_shapes=[pltpu.VMEM((2 * RANK, width), jnp.bfloat16)] * 2,
        name="rank_part",
    )(meta, slot, segment, tokens, *got)


def query_kernel(meta_ref, slot_ref, segment_ref, base_ref, *refs):
    parts, got, (q_ref, up) = refs[0:4], refs[4:12], refs[12:]

    def store(k, rank, block):
        for start in (k * RANK + rank, (3 - k) * RANK + rank):
            up[start:start + RANK // 2, :] = block

    keep_items(meta_ref, slot_ref, segment_ref, got, 1, store)
    cut = meta_ref[1]
    total = functools.reduce(jnp.add, [p[...].astype(jnp.float32) for p in parts])
    half = total.shape[0]
    row = lax.broadcasted_iota(jnp.int32, (half, 2 * RANK), 0)
    lane = lax.broadcasted_iota(jnp.int32, (half, 2 * RANK), 1)
    left = lane < RANK
    zero = jnp.zeros_like(total)

    def masked(keep):
        return jnp.where(keep, total, zero).astype(jnp.bfloat16)

    first, second = row < cut, row + half < cut
    lhs = jnp.concatenate(
        [
            jnp.concatenate([masked(left & first), masked(left & ~first)], axis=1),
            jnp.concatenate([masked(~left & ~second), masked(~left & second)], axis=1),
        ],
        axis=0,
    )
    tiles = 2 * half // TILE
    for t in range(tiles):
        rows = slice(t * TILE, (t + 1) * TILE)
        lora = jnp.dot(lhs[rows], up[...], preferred_element_type=jnp.float32)
        q = (base_ref[rows, :].astype(jnp.float32) + adapter_scale * lora).astype(jnp.bfloat16)
        for p in range(2):
            for h in range(HEADS):
                at = ((2 * t + p) * HEADS + h) * PART
                q_ref[at:at + PART, :] = q[p * PART:(p + 1) * PART, h * HEAD_SIZE:(h + 1) * HEAD_SIZE]
    end = tiles * STEP_ROWS
    q_ref[end:end + PART_ROWS, :] = jnp.zeros((PART_ROWS, HEAD_SIZE), jnp.bfloat16)
    start = pl.multiple_of(cut // PART * PART_ROWS, PART_ROWS)
    q_ref[end:end + STEP_ROWS, :] = q_ref[pl.ds(start, STEP_ROWS), :]


def queries(meta, slot, segment, base, parts, got):
    smem = pl.BlockSpec(memory_space=pltpu.SMEM)
    vmem = pl.BlockSpec(memory_space=pltpu.VMEM)
    rows, width = base.shape
    return pl.pallas_call(
        query_kernel,
        out_shape=jax.ShapeDtypeStruct((rows * HEADS + STEP_ROWS, HEAD_SIZE), jnp.bfloat16),
        in_specs=[smem] * 3 + [vmem] * 13,
        out_specs=vmem,
        scratch_shapes=[
            pltpu.VMEM((4 * RANK, width), jnp.bfloat16),
        ],
        compiler_params=pltpu.CompilerParams(vmem_limit_bytes=VMEM_LIMIT),
        name="queries",
    )(meta, slot, segment, base, *parts, *got)


def attend_kernel(blocks, *refs):
    meta_ref, ids_ref, q_ref, span_ref, prev_ref, cache_ref, out_ref = refs[:7]
    (k_sc, v_sc, count_sc, double_steps, steps, half_steps, m_sc, al_sc,
     d_even, d_odd, h_even, h_odd, k_sem, v_sem) = refs[7:]
    s_even, s_odd = d_even.at[:, 0:GROUP * PAGE], d_odd.at[:, 0:GROUP * PAGE]
    rows_all = q_ref.shape[0] - STEP_ROWS
    tiles = rows_all // STEP_ROWS
    keys_step = GROUP * PAGE
    groups = k_sc.shape[0] // 2 // keys_step
    own_rows = cache_ref.shape[0] // blocks
    own_pages = own_rows // (2 * PAGE)
    seg_a, cut = meta_ref[0], meta_ref[1]

    def rows_at(start, count=STEP_ROWS):
        return pl.ds(pl.multiple_of(start, PART_ROWS), count)

    def keys_at(g, count):
        return pl.ds(pl.multiple_of(g * keys_step, keys_step), count)

    def score(i, s_ref, listed):
        at = jnp.minimum(listed[2 * i], rows_all)
        s_ref[...] = lax.dot_general(
            q_ref[rows_at(at, s_ref.shape[0]), :],
            k_sc[keys_at(listed[2 * i + 1], s_ref.shape[1]), :],
            (((1,), (1,)), ((), ())),
            preferred_element_type=jnp.float32,
        )

    def soften(i, s_ref, listed):
        rows = rows_at(listed[2 * i], s_ref.shape[0])
        keys = keys_at(listed[2 * i + 1], s_ref.shape[1])
        parts = [s_ref[:, j * 128:(j + 1) * 128] for j in range(s_ref.shape[1] // 128)]
        peak = jnp.max(functools.reduce(jnp.maximum, parts), axis=1, keepdims=True) * LOG_SCALE
        old = m_sc[rows, :]
        new = jnp.maximum(old, peak)
        fade = jnp.exp2(old - new)
        weights = jnp.concatenate(
            [jnp.exp2(s * LOG_SCALE - new).astype(jnp.bfloat16) for s in parts], axis=1
        )
        added = jnp.dot(weights, v_sc[keys, :], preferred_element_type=jnp.float32)
        m_sc[rows, :] = new
        al_sc[rows, 0:128] = al_sc[rows, 0:128] * fade + added[:, 0:128]
        al_sc[rows, 128:256] = al_sc[rows, 128:256] * fade + added[:, 128:256]

    def weigh(i, s_ref, listed):
        rows = rows_at(listed[2 * i], s_ref.shape[0])
        keys = keys_at(listed[2 * i + 1], s_ref.shape[1])
        top = m_sc[rows, :]
        weights = jnp.concatenate(
            [
                jnp.exp2(s_ref[:, j * 128:(j + 1) * 128] * LOG_SCALE - top).astype(jnp.bfloat16)
                for j in range(s_ref.shape[1] // 128)
            ],
            axis=1,
        )
        al_sc[rows, :] += jnp.dot(weights, v_sc[keys, :], preferred_element_type=jnp.float32)

    span_keys = jnp.concatenate([prev_ref[0:256, :], span_ref[0:256, :]], axis=0)
    span_values = jnp.concatenate(
        [
            jnp.concatenate([prev_ref[256:512, :], span_ref[256:512, :]], axis=0),
            jnp.ones((512, 128), jnp.bfloat16),
        ],
        axis=1,
    )

    before = jnp.max(prev_ref[512:528, :].astype(jnp.float32)).astype(jnp.int32)
    prev_cut = jnp.where(seg_a == 0, 256, before)

    def token_of(start, count, lanes):
        row = lax.broadcasted_iota(jnp.int32, (count, lanes), 0)
        return (start // PART_ROWS + row // PART_ROWS) * PART + row % PART

    def span_tile(t, first, end):
        rows = rows_at(t * STEP_ROWS)
        count = end - first
        scores = lax.dot_general(
            q_ref[rows, :],
            span_keys[first:end],
            (((1,), (1,)), ((), ())),
            preferred_element_type=jnp.float32,
        )
        token = token_of(t * STEP_ROWS, STEP_ROWS, count)
        key = lax.broadcasted_iota(jnp.int32, (STEP_ROWS, count), 1) + (first - 256)
        in_a = token < cut
        keep = ((key < 0) & in_a & (key + 256 >= prev_cut)) | (
            (key >= 0) & (key <= token) & ((key < cut) == in_a)
        )
        scores = jnp.where(keep, scores * LOG_SCALE, NEG)
        peak = jnp.max(scores, axis=1, keepdims=True)
        weights = jnp.exp2(scores - peak).astype(jnp.bfloat16)
        m_sc[rows, :] = jnp.broadcast_to(peak, (STEP_ROWS, 128))
        al_sc[rows, :] = jnp.dot(weights, span_values[first:end], preferred_element_type=jnp.float32)

    count_sc[0] = 0
    count_sc[1] = 0

    def page_copies(d, page, slot):
        here = pl.ds(pl.multiple_of(slot * PAGE, PAGE), PAGE)
        at = pl.multiple_of(d * own_rows + page * PAGE, 16)
        keys = pltpu.make_async_copy(cache_ref.at[pl.ds(at, PAGE)], k_sc.at[here], k_sem)
        at = pl.multiple_of(d * own_rows + (own_pages + page) * PAGE, 16)
        values = pltpu.make_async_copy(
            cache_ref.at[pl.ds(at, PAGE)], v_sc.at[here, pl.ds(0, 128)], v_sem
        )
        return keys, values

    @pl.loop(0, blocks * own_pages)
    def _(i):
        d, page = i // own_pages, lax.rem(i, own_pages)
        which = ids_ref[i] - seg_a

        @pl.when((which == 0) | (which == 1))
        def _():
            n = count_sc[which]
            for c in page_copies(d, page, which * groups * GROUP + n):
                c.start()
            count_sc[which] = n + 1

    low = cut // PART
    mixed_start = low * PART_ROWS
    mixed = rows_at(mixed_start)

    def begin():
        for t in range(tiles):
            end = 256 + 128 * (t * TILE // 128 + 1)
            if t == 0:
                span_tile(t, 0, end)
            else:
                @pl.when(t * TILE < cut)
                def _(t=t, end=end):
                    span_tile(t, 0, end)

                @pl.when(t * TILE >= cut)
                def _(t=t, end=end):
                    span_tile(t, 256, end)

        m_sc[rows_all:rows_all + STEP_ROWS, :] = m_sc[mixed, :]
        al_sc[rows_all:rows_all + STEP_ROWS, :] = al_sc[mixed, :]

    begin()

    @pl.loop(0, count_sc[0] + count_sc[1])
    def _(i):
        for c in page_copies(0, 0, 0):
            c.wait()

    count_sc[2] = 0
    count_sc[3] = 0
    count_sc[4] = 0
    for side in range(2):
        n = count_sc[side]
        full = (n + GROUP - 1) // GROUP
        base = side * groups * keys_step

        @pl.loop(0, n)
        def _(i, base=base):
            there = pl.ds(pl.multiple_of(base + i * PAGE, PAGE), PAGE)
            v_sc[there, 128:256] = jnp.ones((PAGE, 128), jnp.bfloat16)

        @pl.loop(n, full * GROUP)
        def _(i, base=base):
            there = pl.ds(pl.multiple_of(base + i * PAGE, PAGE), PAGE)
            k_sc[there, :] = k_sc[base:base + PAGE, :]
            v_sc[there, :] = jnp.zeros((PAGE, 256), jnp.bfloat16)

        parts = (cut + PART - 1) // PART if side == 0 else 2 * tiles - low
        odd = lax.rem(parts, 2)

        def add_steps(listed, counter, g, side=side, parts=parts, odd=odd):
            @pl.loop(0, parts // 2)
            def _(t):
                c = count_sc[counter]
                start = t * STEP_ROWS
                if side == 1:
                    start = start + (low + odd) * PART_ROWS
                    start = jnp.where((t == 0) & (odd == 0), rows_all, start)
                listed[2 * c] = start
                listed[2 * c + 1] = side * groups + g
                count_sc[counter] = c + 1

        @pl.loop(0, full // 2)
        def _(g):
            add_steps(double_steps, 4, 2 * g)

        @pl.when(lax.rem(full, 2) == 1)
        def _():
            add_steps(steps, 2, full - 1)

        @pl.loop(0, full)
        def _(g, side=side, parts=parts, odd=odd):
            @pl.when(odd == 1)
            def _():
                c = count_sc[3]
                half_steps[2 * c] = rows_all if side == 1 else (parts - 1) * PART_ROWS
                half_steps[2 * c + 1] = side * groups + g
                count_sc[3] = c + 1

    lists = ((double_steps, 4, d_even, d_odd), (steps, 2, s_even, s_odd), (half_steps, 3, h_even, h_odd))
    for listed, n, _, _ in lists:
        n = count_sc[n]
        for e in range(2):
            listed[2 * (n + e)] = rows_all + STEP_ROWS
            listed[2 * (n + e) + 1] = 0

    def run(total, listed, even_ref, odd_ref, finish):
        @pl.when(total > 0)
        def _():
            score(0, even_ref, listed)

        @pl.loop(0, (total + 1) // 2)
        def _(j):
            score(2 * j + 1, odd_ref, listed)
            finish(2 * j, even_ref, listed)
            score(2 * j + 2, even_ref, listed)
            finish(2 * j + 1, odd_ref, listed)

    for listed, n, even_ref, odd_ref in lists:
        run(count_sc[n], listed, even_ref, odd_ref, weigh)

    used = al_sc[0:rows_all + STEP_ROWS, 128:256]
    beyond = jnp.max(jnp.where(used <= LARGEST_SUM, 0.0, 1.0))

    @pl.when(beyond > 0.5)
    def _():
        begin()
        for listed, n, even_ref, odd_ref in lists:
            run(count_sc[n], listed, even_ref, odd_ref, soften)


    row = lax.broadcasted_iota(jnp.int32, (STEP_ROWS, 128), 0)
    moved = (token_of(mixed_start, STEP_ROWS, 128) >= cut) & ((row < PART_ROWS) | (lax.rem(low, 2) == 0))
    for c in range(2):
        cols = slice(c * 128, (c + 1) * 128)
        al_sc[mixed, cols] = jnp.where(
            moved, al_sc[rows_all:rows_all + STEP_ROWS, cols], al_sc[mixed, cols]
        )
    for p in range(2 * tiles):
        for h in range(HEADS):
            at = (p * HEADS + h) * PART
            out = al_sc[at:at + PART, 0:128] / al_sc[at:at + PART, 128:256]
            out_ref[p * PART:(p + 1) * PART, h * 128:(h + 1) * 128] = out.astype(jnp.bfloat16)


def attend(meta, ids, q, span, prev, cache, blocks):
    rows = q.shape[0] - STEP_ROWS
    tiles = rows // STEP_ROWS
    groups = -(-ids.shape[0] // GROUP)
    vmem = pl.BlockSpec(memory_space=pltpu.VMEM)
    return pl.pallas_call(
        functools.partial(attend_kernel, blocks),
        out_shape=jax.ShapeDtypeStruct((rows // HEADS, HEADS * HEAD_SIZE), jnp.bfloat16),
        in_specs=[pl.BlockSpec(memory_space=pltpu.SMEM)] * 2
        + [vmem] * 3
        + [pl.BlockSpec(memory_space=pl.ANY)],
        out_specs=vmem,
        scratch_shapes=[
            pltpu.VMEM((2 * groups * GROUP * PAGE, 128), jnp.bfloat16),
            pltpu.VMEM((2 * groups * GROUP * PAGE, 256), jnp.bfloat16),
            pltpu.SMEM((5,), jnp.int32),
            pltpu.SMEM((2 * ((tiles + 1) * (groups + 1) + 4),), jnp.int32),
            pltpu.SMEM((2 * (2 * (tiles + 1) + 4),), jnp.int32),
            pltpu.SMEM((2 * (2 * (groups + 1) + 4),), jnp.int32),
            pltpu.VMEM((rows + 2 * STEP_ROWS, 128), jnp.float32),
            pltpu.VMEM((rows + 2 * STEP_ROWS, 256), jnp.float32),
            pltpu.VMEM((STEP_ROWS, 2 * GROUP * PAGE), jnp.float32),
            pltpu.VMEM((STEP_ROWS, 2 * GROUP * PAGE), jnp.float32),
            pltpu.VMEM((PART_ROWS, GROUP * PAGE), jnp.float32),
            pltpu.VMEM((PART_ROWS, GROUP * PAGE), jnp.float32),
            pltpu.SemaphoreType.DMA(()),
            pltpu.SemaphoreType.DMA(()),
        ],
        compiler_params=pltpu.CompilerParams(vmem_limit_bytes=VMEM_LIMIT),
        name="attend",
    )(meta, ids, q, span, prev, cache)


def per_device(
    tokens_in,
    base_queries,
    fresh_keys,
    fresh_values,
    cached_key_rows,
    cached_value_rows,
    adapter_store,
    adapter_slot,
    segment_adapter,
    token_request,
    cache_doc,
):
    seg_a = token_request[0]
    cut = jnp.sum((token_request == seg_a).astype(jnp.int32))
    meta = jnp.stack([seg_a, cut])

    own = jnp.concatenate([cached_key_rows, cached_value_rows], axis=0)
    cache = lax.all_gather(own, "ctx", axis=0, tiled=True)

    mid = RANK // 2
    width = adapter_store.shape[3]
    pages = cache_doc.shape[0]
    lane = jnp.arange(width, dtype=jnp.int32)
    docs = jnp.tile(cache_doc, width // pages)
    docs = jnp.where(lane // pages == lax.axis_index("ctx"), docs, 0).astype(jnp.bfloat16)
    span = jnp.concatenate(
        [fresh_keys, fresh_values, jnp.broadcast_to(cut.astype(jnp.bfloat16), (16, 128))], axis=0
    )
    rows, prev = ring_rows(
        jnp.concatenate(
            [
                adapter_store[:, :, :mid].reshape(-1, width),
                jnp.broadcast_to(docs[None], (16, width)),
            ],
            axis=0,
        ),
        adapter_store[:, :, mid:].reshape(-1, width),
        span,
    )

    ids = (meta, adapter_slot, segment_adapter)
    got = hand_over(pick(*ids, rows))
    owners = functools.reduce(jnp.add, [g[2 * RANK, :SIDE * SIDE * pages].astype(jnp.int32) for g in got[:4]])

    acts = rank_part(*ids, tokens_in, got)
    pair = pull_tp(acts, 0, 1)
    acts = (acts.astype(jnp.float32) + pair.astype(jnp.float32)).astype(jnp.bfloat16)
    parts = [acts] + [pull_tp(acts, dz, 0) for dz in (1, 2, 3)]
    query = queries(*ids, base_queries, parts, got)
    return attend(meta, owners, query, span, prev, cache, SIDE * SIDE)


def solution(mesh):
    in_specs = (
        P("ctx", "tp"),
        P("ctx", "tp"),
        P("ctx", "tp"),
        P("ctx", "tp"),
        P("ctx", "tp"),
        P("ctx", "tp"),
        P("ctx", None, None, "tp"),
        P(),
        P(),
        P("ctx"),
        P("ctx"),
    )
    out_specs = P("ctx", "tp")
    return jax.shard_map(
        per_device, mesh=mesh, in_specs=in_specs, out_specs=out_specs, check_vma=False
    )
```

```python
import functools
import math

import jax
import jax.numpy as jnp
from jax import lax
from jax.experimental import pallas as pl
from jax.experimental.pallas import tpu as pltpu
from jax.sharding import PartitionSpec as P

HEAD_SIZE = 128
PAGE = 128
SIDE = 4
RANK = 64
HEADS = 8
TILE = 64
PART = TILE // 2
GROUP = 8
STEP_ROWS = TILE * HEADS
PART_ROWS = PART * HEADS
NEG = -1e30
LARGEST_SUM = 2.0**90
VMEM_LIMIT = 56 * 1024 * 1024
LOG_SCALE = math.log2(math.e) / math.sqrt(HEAD_SIZE)

adapter_scale = 2.0


def pull(block, dx, dy):
    route = []
    for i in range(SIDE * SIDE):
        y, x = divmod(i, SIDE)
        route.append((((y + dy) % SIDE) * SIDE + (x + dx) % SIDE, i))
    return lax.ppermute(block, "ctx", route)


def pull_tp(block, dz, dc):
    route = []
    for i in range(2 * SIDE):
        z, c = divmod(i, 2)
        route.append((((z + dz) % SIDE) * 2 + (c ^ dc), i))
    return lax.ppermute(block, "tp", route)


def stored_row(slot_ref, segment_ref, segment):
    return slot_ref[segment_ref[segment]]


def place(index, along_x):
    y, x = index // SIDE, lax.rem(index, SIDE)
    return (x, y) if along_x else (y, x)


def pick_kernel(meta_ref, slot_ref, segment_ref, *refs):
    bufs, outs, sems, owners, owner_sems = refs[0:10], refs[10:18], refs[18], refs[19], refs[20]
    me = meta_ref[0]
    stored = 4 * RANK
    found_at = ((bufs[0], stored), (bufs[1], stored), (bufs[2], stored), (bufs[4], stored // 2))
    owner_copies = [
        pltpu.make_async_copy(buf.at[pl.ds(start, 16)], owners.at[n], owner_sems.at[n])
        for n, (buf, start) in enumerate(found_at)
    ]
    for c in owner_copies:
        c.start()
    for f, along_x in enumerate((True, False)):
        along, across = place(me, along_x)
        for d in range(SIDE):
            there = lax.rem(across + d, SIDE)
            dest = there * SIDE + along if along_x else along * SIDE + there
            for k in range(2):
                row = stored_row(slot_ref, segment_ref, dest + k)
                owner_along, _ = place(row // 4, along_x)
                ring = lax.rem(owner_along - along + SIDE, SIDE)
                index = lax.rem(row, 4)
                cases = (
                    (ring == 0, index),
                    (ring == 1, index),
                    (ring == 3, index),
                    ((ring == 2) & (index < 2), index),
                    ((ring == 2) & (index >= 2), index - 2),
                )
                for b, (found, at) in enumerate(cases):
                    @pl.when(found)
                    def _():
                        pltpu.make_async_copy(
                            bufs[f * 5 + b].at[pl.ds(pl.multiple_of(at * RANK, RANK), RANK)],
                            outs[f * 4 + d].at[pl.ds(k * RANK, RANK)],
                            sems.at[f * 8 + d * 2 + k],
                        ).start()
    for c in owner_copies:
        c.wait()
    total = functools.reduce(jnp.add, [owners[n].astype(jnp.float32) for n in range(SIDE)])
    for d in range(SIDE):
        outs[d][2 * RANK:, :] = total.astype(jnp.bfloat16)
    for f in range(2):
        for d in range(SIDE):
            for k in range(2):
                pltpu.make_async_copy(
                    bufs[f * 5].at[pl.ds(0, RANK)],
                    outs[f * 4 + d].at[pl.ds(k * RANK, RANK)],
                    sems.at[f * 8 + d * 2 + k],
                ).wait()


def pick(meta, slot, segment, bufs):
    width = bufs[0].shape[1]
    with_owners = jax.ShapeDtypeStruct((2 * RANK + 16, width), jnp.bfloat16)
    without = jax.ShapeDtypeStruct((2 * RANK, width), jnp.bfloat16)
    smem = pl.BlockSpec(memory_space=pltpu.SMEM)
    return pl.pallas_call(
        pick_kernel,
        out_shape=[with_owners] * 4 + [without] * 4,
        in_specs=[smem] * 3 + [pl.BlockSpec(memory_space=pl.ANY)] * 10,
        out_specs=[pl.BlockSpec(memory_space=pltpu.VMEM)] * 8,
        scratch_shapes=[
            pltpu.SemaphoreType.DMA((16,)),
            pltpu.VMEM((SIDE, 16, width), jnp.bfloat16),
            pltpu.SemaphoreType.DMA((SIDE,)),
        ],
        name="pick_items",
    )(meta, slot, segment, *bufs)


def ring_rows(raw_x, raw_y, span):
    after_x, before_x = pull(raw_x, 1, 0), pull(raw_x, -1, 0)
    after_y, before_y = pull(raw_y, 0, 1), pull(raw_y, 0, -1)
    prev = lax.ppermute(span, "ctx", [(i - 1, i) for i in range(1, SIDE * SIDE)])
    before_x, prev = lax.optimization_barrier((before_x, prev))
    half = raw_y.shape[0] // 2
    return [
        raw_x, after_x, before_x, pull(after_x[:half], 1, 0), pull(before_x[half:], -1, 0),
        raw_y, after_y, before_y, pull(after_y[:half], 0, 1), pull(before_y[half:], 0, -1),
    ], prev


def hand_over(items):
    return [
        items[0], pull(items[3], 0, 1), pull(items[2], 0, 2), pull(items[1], 0, -1),
        items[4], pull(items[7], 1, 0), pull(items[6], 2, 0), pull(items[5], -1, 0),
    ]


def keep_items(meta_ref, slot_ref, segment_ref, got, part, store):
    me = meta_ref[0]
    half = RANK // 2
    for f, along_x in enumerate((True, False)):
        _, across = place(me, along_x)
        for k in range(2):
            row = stored_row(slot_ref, segment_ref, me + k)
            _, owner_across = place(row // 4, along_x)
            source = lax.rem(owner_across - across + SIDE, SIDE)
            block = slice(k * RANK + part * half, k * RANK + (part + 1) * half)
            for d in range(SIDE):
                @pl.when(source == d)
                def _():
                    store(k, f * half, got[f * 4 + d][block, :])


def rank_kernel(meta_ref, slot_ref, segment_ref, tokens_ref, *refs):
    got, (out_ref, down, swapped) = refs[0:8], refs[8:]

    def store(k, rank, block):
        down[k * RANK + rank:k * RANK + rank + RANK // 2, :] = block
        other = (1 - k) * RANK + rank
        swapped[other:other + RANK // 2, :] = block

    keep_items(meta_ref, slot_ref, segment_ref, got, 0, store)
    cut = meta_ref[1]
    half = out_ref.shape[0]
    dims = (((1,), (1,)), ((), ()))
    tokens = tokens_ref[...]
    straight = lax.dot_general(tokens, down[...], dims, preferred_element_type=jnp.float32)
    crossed = lax.dot_general(tokens, swapped[...], dims, preferred_element_type=jnp.float32)
    row = lax.broadcasted_iota(jnp.int32, (half, 2 * RANK), 0)
    lane = lax.broadcasted_iota(jnp.int32, (half, 2 * RANK), 1)
    top = jnp.where(row < cut, straight[:half], crossed[:half])
    bottom = jnp.where(row + half < cut, crossed[half:], straight[half:])
    out_ref[...] = jnp.where(lane < RANK, top, bottom).astype(jnp.bfloat16)


def rank_part(meta, slot, segment, tokens, got):
    smem = pl.BlockSpec(memory_space=pltpu.SMEM)
    vmem = pl.BlockSpec(memory_space=pltpu.VMEM)
    rows, width = tokens.shape
    return pl.pallas_call(
        rank_kernel,
        out_shape=jax.ShapeDtypeStruct((rows // 2, 2 * RANK), jnp.bfloat16),
        in_specs=[smem] * 3 + [vmem] * 9,
        out_specs=vmem,
        scratch_shapes=[pltpu.VMEM((2 * RANK, width), jnp.bfloat16)] * 2,
        name="rank_part",
    )(meta, slot, segment, tokens, *got)


def query_kernel(meta_ref, slot_ref, segment_ref, base_ref, *refs):
    parts, got, (q_ref, up) = refs[0:4], refs[4:12], refs[12:]

    def store(k, rank, block):
        for start in (k * RANK + rank, (3 - k) * RANK + rank):
            up[start:start + RANK // 2, :] = block

    keep_items(meta_ref, slot_ref, segment_ref, got, 1, store)
    cut = meta_ref[1]
    total = functools.reduce(jnp.add, [p[...].astype(jnp.float32) for p in parts])
    half = total.shape[0]
    row = lax.broadcasted_iota(jnp.int32, (half, 2 * RANK), 0)
    lane = lax.broadcasted_iota(jnp.int32, (half, 2 * RANK), 1)
    left = lane < RANK
    zero = jnp.zeros_like(total)

    def masked(keep):
        return jnp.where(keep, total, zero).astype(jnp.bfloat16)

    first, second = row < cut, row + half < cut
    lhs = jnp.concatenate(
        [
            jnp.concatenate([masked(left & first), masked(left & ~first)], axis=1),
            jnp.concatenate([masked(~left & ~second), masked(~left & second)], axis=1),
        ],
        axis=0,
    )
    tiles = 2 * half // TILE
    for t in range(tiles):
        rows = slice(t * TILE, (t + 1) * TILE)
        lora = jnp.dot(lhs[rows], up[...], preferred_element_type=jnp.float32)
        q = (base_ref[rows, :].astype(jnp.float32) + adapter_scale * lora).astype(jnp.bfloat16)
        for p in range(2):
            for h in range(HEADS):
                at = ((2 * t + p) * HEADS + h) * PART
                q_ref[at:at + PART, :] = q[p * PART:(p + 1) * PART, h * HEAD_SIZE:(h + 1) * HEAD_SIZE]
    end = tiles * STEP_ROWS
    q_ref[end:end + PART_ROWS, :] = jnp.zeros((PART_ROWS, HEAD_SIZE), jnp.bfloat16)
    start = pl.multiple_of(cut // PART * PART_ROWS, PART_ROWS)
    q_ref[end:end + STEP_ROWS, :] = q_ref[pl.ds(start, STEP_ROWS), :]


def queries(meta, slot, segment, base, parts, got):
    smem = pl.BlockSpec(memory_space=pltpu.SMEM)
    vmem = pl.BlockSpec(memory_space=pltpu.VMEM)
    rows, width = base.shape
    return pl.pallas_call(
        query_kernel,
        out_shape=jax.ShapeDtypeStruct((rows * HEADS + STEP_ROWS, HEAD_SIZE), jnp.bfloat16),
        in_specs=[smem] * 3 + [vmem] * 13,
        out_specs=vmem,
        scratch_shapes=[
            pltpu.VMEM((4 * RANK, width), jnp.bfloat16),
        ],
        compiler_params=pltpu.CompilerParams(vmem_limit_bytes=VMEM_LIMIT),
        name="queries",
    )(meta, slot, segment, base, *parts, *got)


def attend_kernel(blocks, *refs):
    meta_ref, ids_ref, q_ref, span_ref, prev_ref, cache_ref, out_ref = refs[:7]
    (k_sc, v_sc, count_sc, double_steps, steps, half_steps, m_sc, al_sc,
     d_even, d_odd, h_even, h_odd, k_sem, v_sem) = refs[7:]
    s_even, s_odd = d_even.at[:, 0:GROUP * PAGE], d_odd.at[:, 0:GROUP * PAGE]
    rows_all = q_ref.shape[0] - STEP_ROWS
    tiles = rows_all // STEP_ROWS
    keys_step = GROUP * PAGE
    groups = k_sc.shape[0] // 2 // keys_step
    own_rows = cache_ref.shape[0] // blocks
    own_pages = own_rows // (2 * PAGE)
    seg_a, cut = meta_ref[0], meta_ref[1]

    def rows_at(start, count=STEP_ROWS):
        return pl.ds(pl.multiple_of(start, PART_ROWS), count)

    def keys_at(g, count):
        return pl.ds(pl.multiple_of(g * keys_step, keys_step), count)

    def score(i, s_ref, listed):
        at = jnp.minimum(listed[2 * i], rows_all)
        s_ref[...] = lax.dot_general(
            q_ref[rows_at(at, s_ref.shape[0]), :],
            k_sc[keys_at(listed[2 * i + 1], s_ref.shape[1]), :],
            (((1,), (1,)), ((), ())),
            preferred_element_type=jnp.float32,
        )

    def soften(i, s_ref, listed):
        rows = rows_at(listed[2 * i], s_ref.shape[0])
        keys = keys_at(listed[2 * i + 1], s_ref.shape[1])
        parts = [s_ref[:, j * 128:(j + 1) * 128] for j in range(s_ref.shape[1] // 128)]
        peak = jnp.max(functools.reduce(jnp.maximum, parts), axis=1, keepdims=True) * LOG_SCALE
        old = m_sc[rows, :]
        new = jnp.maximum(old, peak)
        fade = jnp.exp2(old - new)
        weights = jnp.concatenate(
            [jnp.exp2(s * LOG_SCALE - new).astype(jnp.bfloat16) for s in parts], axis=1
        )
        added = jnp.dot(weights, v_sc[keys, :], preferred_element_type=jnp.float32)
        m_sc[rows, :] = new
        al_sc[rows, 0:128] = al_sc[rows, 0:128] * fade + added[:, 0:128]
        al_sc[rows, 128:256] = al_sc[rows, 128:256] * fade + added[:, 128:256]

    def weigh(i, s_ref, listed):
        rows = rows_at(listed[2 * i], s_ref.shape[0])
        keys = keys_at(listed[2 * i + 1], s_ref.shape[1])
        top = m_sc[rows, :]
        weights = jnp.concatenate(
            [
                jnp.exp2(s_ref[:, j * 128:(j + 1) * 128] * LOG_SCALE - top).astype(jnp.bfloat16)
                for j in range(s_ref.shape[1] // 128)
            ],
            axis=1,
        )
        al_sc[rows, :] += jnp.dot(weights, v_sc[keys, :], preferred_element_type=jnp.float32)

    span_keys = jnp.concatenate([prev_ref[0:256, :], span_ref[0:256, :]], axis=0)
    span_values = jnp.concatenate(
        [
            jnp.concatenate([prev_ref[256:512, :], span_ref[256:512, :]], axis=0),
            jnp.ones((512, 128), jnp.bfloat16),
        ],
        axis=1,
    )

    before = jnp.max(prev_ref[512:528, :].astype(jnp.float32)).astype(jnp.int32)
    prev_cut = jnp.where(seg_a == 0, 256, before)

    def token_of(start, count, lanes):
        row = lax.broadcasted_iota(jnp.int32, (count, lanes), 0)
        return (start // PART_ROWS + row // PART_ROWS) * PART + row % PART

    def span_tile(t, first, end):
        rows = rows_at(t * STEP_ROWS)
        count = end - first
        scores = lax.dot_general(
            q_ref[rows, :],
            span_keys[first:end],
            (((1,), (1,)), ((), ())),
            preferred_element_type=jnp.float32,
        )
        token = token_of(t * STEP_ROWS, STEP_ROWS, count)
        key = lax.broadcasted_iota(jnp.int32, (STEP_ROWS, count), 1) + (first - 256)
        in_a = token < cut
        keep = ((key < 0) & in_a & (key + 256 >= prev_cut)) | (
            (key >= 0) & (key <= token) & ((key < cut) == in_a)
        )
        scores = jnp.where(keep, scores * LOG_SCALE, NEG)
        peak = jnp.max(scores, axis=1, keepdims=True)
        weights = jnp.exp2(scores - peak).astype(jnp.bfloat16)
        m_sc[rows, :] = jnp.broadcast_to(peak, (STEP_ROWS, 128))
        al_sc[rows, :] = jnp.dot(weights, span_values[first:end], preferred_element_type=jnp.float32)

    count_sc[0] = 0
    count_sc[1] = 0

    def page_copies(d, page, slot):
        here = pl.ds(pl.multiple_of(slot * PAGE, PAGE), PAGE)
        at = pl.multiple_of(d * own_rows + page * PAGE, 16)
        keys = pltpu.make_async_copy(cache_ref.at[pl.ds(at, PAGE)], k_sc.at[here], k_sem)
        at = pl.multiple_of(d * own_rows + (own_pages + page) * PAGE, 16)
        values = pltpu.make_async_copy(
            cache_ref.at[pl.ds(at, PAGE)], v_sc.at[here, pl.ds(0, 128)], v_sem
        )
        return keys, values

    @pl.loop(0, blocks * own_pages)
    def _(i):
        d, page = i // own_pages, lax.rem(i, own_pages)
        which = ids_ref[i] - seg_a

        @pl.when((which == 0) | (which == 1))
        def _():
            n = count_sc[which]
            for c in page_copies(d, page, which * groups * GROUP + n):
                c.start()
            count_sc[which] = n + 1

    low = cut // PART
    mixed_start = low * PART_ROWS
    mixed = rows_at(mixed_start)

    def begin():
        for t in range(tiles):
            end = 256 + 128 * (t * TILE // 128 + 1)
            if t == 0:
                span_tile(t, 0, end)
            else:
                @pl.when(t * TILE < cut)
                def _(t=t, end=end):
                    span_tile(t, 0, end)

                @pl.when(t * TILE >= cut)
                def _(t=t, end=end):
                    span_tile(t, 256, end)

        m_sc[rows_all:rows_all + STEP_ROWS, :] = m_sc[mixed, :]
        al_sc[rows_all:rows_all + STEP_ROWS, :] = al_sc[mixed, :]

    begin()

    @pl.loop(0, count_sc[0] + count_sc[1])
    def _(i):
        for c in page_copies(0, 0, 0):
            c.wait()

    count_sc[2] = 0
    count_sc[3] = 0
    count_sc[4] = 0
    for side in range(2):
        n = count_sc[side]
        full = (n + GROUP - 1) // GROUP
        base = side * groups * keys_step

        @pl.loop(0, n)
        def _(i, base=base):
            there = pl.ds(pl.multiple_of(base + i * PAGE, PAGE), PAGE)
            v_sc[there, 128:256] = jnp.ones((PAGE, 128), jnp.bfloat16)

        @pl.loop(n, full * GROUP)
        def _(i, base=base):
            there = pl.ds(pl.multiple_of(base + i * PAGE, PAGE), PAGE)
            k_sc[there, :] = k_sc[base:base + PAGE, :]
            v_sc[there, :] = jnp.zeros((PAGE, 256), jnp.bfloat16)

        parts = (cut + PART - 1) // PART if side == 0 else 2 * tiles - low
        odd = lax.rem(parts, 2)

        def add_steps(listed, counter, g, side=side, parts=parts, odd=odd):
            @pl.loop(0, parts // 2)
            def _(t):
                c = count_sc[counter]
                start = t * STEP_ROWS
                if side == 1:
                    start = start + (low + odd) * PART_ROWS
                    start = jnp.where((t == 0) & (odd == 0), rows_all, start)
                listed[2 * c] = start
                listed[2 * c + 1] = side * groups + g
                count_sc[counter] = c + 1

        @pl.loop(0, full // 2)
        def _(g):
            add_steps(double_steps, 4, 2 * g)

        @pl.when(lax.rem(full, 2) == 1)
        def _():
            add_steps(steps, 2, full - 1)

        @pl.loop(0, full)
        def _(g, side=side, parts=parts, odd=odd):
            @pl.when(odd == 1)
            def _():
                c = count_sc[3]
                half_steps[2 * c] = rows_all if side == 1 else (parts - 1) * PART_ROWS
                half_steps[2 * c + 1] = side * groups + g
                count_sc[3] = c + 1

    lists = ((double_steps, 4, d_even, d_odd), (steps, 2, s_even, s_odd), (half_steps, 3, h_even, h_odd))
    for listed, n, _, _ in lists:
        n = count_sc[n]
        for e in range(2):
            listed[2 * (n + e)] = rows_all + STEP_ROWS
            listed[2 * (n + e) + 1] = 0

    def run(total, listed, even_ref, odd_ref, finish):
        @pl.when(total > 0)
        def _():
            score(0, even_ref, listed)

        @pl.loop(0, total // 2)
        def _(j):
            score(2 * j + 1, odd_ref, listed)
            finish(2 * j, even_ref, listed)
            score(2 * j + 2, even_ref, listed)
            finish(2 * j + 1, odd_ref, listed)

        @pl.when(lax.rem(total, 2) == 1)
        def _():
            finish(total - 1, even_ref, listed)

    for listed, n, even_ref, odd_ref in lists:
        run(count_sc[n], listed, even_ref, odd_ref, weigh)

    used = al_sc[0:rows_all + STEP_ROWS, 128:256]
    beyond = jnp.max(jnp.where(used <= LARGEST_SUM, 0.0, 1.0))

    @pl.when(beyond > 0.5)
    def _():
        begin()
        for listed, n, even_ref, odd_ref in lists:
            run(count_sc[n], listed, even_ref, odd_ref, soften)


    row = lax.broadcasted_iota(jnp.int32, (STEP_ROWS, 128), 0)
    moved = (token_of(mixed_start, STEP_ROWS, 128) >= cut) & ((row < PART_ROWS) | (lax.rem(low, 2) == 0))
    for c in range(2):
        cols = slice(c * 128, (c + 1) * 128)
        al_sc[mixed, cols] = jnp.where(
            moved, al_sc[rows_all:rows_all + STEP_ROWS, cols], al_sc[mixed, cols]
        )
    for p in range(2 * tiles):
        for h in range(HEADS):
            at = (p * HEADS + h) * PART
            out = al_sc[at:at + PART, 0:128] / al_sc[at:at + PART, 128:256]
            out_ref[p * PART:(p + 1) * PART, h * 128:(h + 1) * 128] = out.astype(jnp.bfloat16)


def attend(meta, ids, q, span, prev, cache, blocks):
    rows = q.shape[0] - STEP_ROWS
    tiles = rows // STEP_ROWS
    groups = -(-ids.shape[0] // GROUP)
    vmem = pl.BlockSpec(memory_space=pltpu.VMEM)
    return pl.pallas_call(
        functools.partial(attend_kernel, blocks),
        out_shape=jax.ShapeDtypeStruct((rows // HEADS, HEADS * HEAD_SIZE), jnp.bfloat16),
        in_specs=[pl.BlockSpec(memory_space=pltpu.SMEM)] * 2
        + [vmem] * 3
        + [pl.BlockSpec(memory_space=pl.ANY)],
        out_specs=vmem,
        scratch_shapes=[
            pltpu.VMEM((2 * groups * GROUP * PAGE, 128), jnp.bfloat16),
            pltpu.VMEM((2 * groups * GROUP * PAGE, 256), jnp.bfloat16),
            pltpu.SMEM((5,), jnp.int32),
            pltpu.SMEM((2 * ((tiles + 1) * (groups + 1) + 4),), jnp.int32),
            pltpu.SMEM((2 * (2 * (tiles + 1) + 4),), jnp.int32),
            pltpu.SMEM((2 * (2 * (groups + 1) + 4),), jnp.int32),
            pltpu.VMEM((rows + 2 * STEP_ROWS, 128), jnp.float32),
            pltpu.VMEM((rows + 2 * STEP_ROWS, 256), jnp.float32),
            pltpu.VMEM((STEP_ROWS, 2 * GROUP * PAGE), jnp.float32),
            pltpu.VMEM((STEP_ROWS, 2 * GROUP * PAGE), jnp.float32),
            pltpu.VMEM((PART_ROWS, GROUP * PAGE), jnp.float32),
            pltpu.VMEM((PART_ROWS, GROUP * PAGE), jnp.float32),
            pltpu.SemaphoreType.DMA(()),
            pltpu.SemaphoreType.DMA(()),
        ],
        compiler_params=pltpu.CompilerParams(vmem_limit_bytes=VMEM_LIMIT),
        name="attend",
    )(meta, ids, q, span, prev, cache)


def per_device(
    tokens_in,
    base_queries,
    fresh_keys,
    fresh_values,
    cached_key_rows,
    cached_value_rows,
    adapter_store,
    adapter_slot,
    segment_adapter,
    token_request,
    cache_doc,
):
    seg_a = token_request[0]
    cut = jnp.sum((token_request == seg_a).astype(jnp.int32))
    meta = jnp.stack([seg_a, cut])

    own = jnp.concatenate([cached_key_rows, cached_value_rows], axis=0)
    cache = lax.all_gather(own, "ctx", axis=0, tiled=True)

    mid = RANK // 2
    width = adapter_store.shape[3]
    pages = cache_doc.shape[0]
    lane = jnp.arange(width, dtype=jnp.int32)
    docs = jnp.tile(cache_doc, width // pages)
    docs = jnp.where(lane // pages == lax.axis_index("ctx"), docs, 0).astype(jnp.bfloat16)
    span = jnp.concatenate(
        [fresh_keys, fresh_values, jnp.broadcast_to(cut.astype(jnp.bfloat16), (16, 128))], axis=0
    )
    rows, prev = ring_rows(
        jnp.concatenate(
            [
                adapter_store[:, :, :mid].reshape(-1, width),
                jnp.broadcast_to(docs[None], (16, width)),
            ],
            axis=0,
        ),
        adapter_store[:, :, mid:].reshape(-1, width),
        span,
    )

    ids = (meta, adapter_slot, segment_adapter)
    got = hand_over(pick(*ids, rows))
    owners = functools.reduce(jnp.add, [g[2 * RANK, :SIDE * SIDE * pages].astype(jnp.int32) for g in got[:4]])

    acts = rank_part(*ids, tokens_in, got)
    pair = pull_tp(acts, 0, 1)
    acts = (acts.astype(jnp.float32) + pair.astype(jnp.float32)).astype(jnp.bfloat16)
    parts = [acts] + [pull_tp(acts, dz, 0) for dz in (1, 2, 3)]
    query = queries(*ids, base_queries, parts, got)
    return attend(meta, owners, query, span, prev, cache, SIDE * SIDE)


def solution(mesh):
    in_specs = (
        P("ctx", "tp"),
        P("ctx", "tp"),
        P("ctx", "tp"),
        P("ctx", "tp"),
        P("ctx", "tp"),
        P("ctx", "tp"),
        P("ctx", None, None, "tp"),
        P(),
        P(),
        P("ctx"),
        P("ctx"),
    )
    out_specs = P("ctx", "tp")
    return jax.shard_map(
        per_device, mesh=mesh, in_specs=in_specs, out_specs=out_specs, check_vma=False
    )
```
